256 devices in a mesh: dp: 64 (over z, x, core), fsdp: 4 (over y).
Axes of the slice: x: 4, y: 4, z: 8, core: 2. Of those that a mesh axis runs over, the one named last changes fastest.
Arguments:
- tokens: bfloat16 [4, 128, 256, 3584], P('fsdp', 'dp'), may hold values from -6 to 6
- lengths: int32 [4, 128], P('fsdp', 'dp'), may hold values from 64 to 256, as said below
- queries: bfloat16 [4, 128, 1792], P('fsdp', 'dp'), may hold values from -6 to 6
- positives: int32 [4, 128], P('fsdp', 'dp'), may hold values from 0 to 127, as said below
- kv_weight: bfloat16 [3584, 512], P('fsdp'), may hold values from -0.09375 to 0.09375
Outputs:
- document_loss: float32 [4, 128], P('fsdp', 'dp')
- grad_tokens: bfloat16 [4, 128, 256, 3584], P('fsdp', 'dp')
- grad_queries: bfloat16 [4, 128, 1792], P('fsdp', 'dp')
- grad_weight: float32 [3584, 512], P(None, ('dp', 'fsdp'))
The draws below stay inside these ranges and needn't reach their ends.
Inputs may be any that keep to these rules, and one draw needn't show every extreme that they name: The lengths of document j of device h and of document j of device h + 64/2 (along dp, same batch, 0 <= h < 32) add up to 320. `positives`: A document is never its own positive.
All inputs are finite; a program needn't handle non-finite values.
Results may differ from the reference program's by a relative error of at most 0.015.
Values may be sent and summed in bfloat16 or wider, within the bound.
No kernel may reach another device: no remote copies, remote signals or barrier semaphores. Data moves between devices by JAX's collectives and lax.ppermute only.
A program may use at most 128 MiB of HBM per device.

```python
import jax
import jax.numpy as jnp
from jax import lax

D = 3584
QH = 14
KVH = 2
HD = 128
DOCS_DEV = 2
BLK = 256
MINLEN = 64
QW = 1792
KVW = 512
NDOCS = 128
GROUPS = 4
N_DP = 64


def draw_lengths(key, part):
    key = jax.random.fold_in(key, 11)
    first_key, second_key = jax.random.split(key)
    half_count = N_DP // 2
    spread = max(BLK // 8, 2)
    centre = jax.random.randint(first_key, (GROUPS, half_count, 1), MINLEN, BLK + 1)
    jitter = jax.random.randint(second_key, (GROUPS, half_count, DOCS_DEV), -spread, spread + 1)
    lower_part = jnp.clip(centre + jitter, MINLEN, BLK)
    lower_part = lower_part.at[:, 0, 0].set(BLK)
    upper_part = BLK + MINLEN - lower_part
    both = jnp.concatenate([lower_part, upper_part], axis=1)
    return both.reshape(GROUPS, NDOCS).astype(jnp.int32)


def draw_positives(key, part):
    key = jax.random.fold_in(key, 23)
    offsets = jax.random.randint(key, (GROUPS, NDOCS), 1, NDOCS)
    return ((jnp.arange(NDOCS)[None, :] + offsets) % NDOCS).astype(jnp.int32)


def block_scale(own_key, dims, pieces, least, high):
    gain = 1.0
    for axis_at, shards_of in pieces:
        heights = jax.random.uniform(jax.random.fold_in(jax.random.fold_in(own_key, 6), axis_at), (shards_of,), jnp.float32, least / len(pieces), high / len(pieces))
        gain = gain * jnp.repeat(jnp.exp(heights), dims[axis_at] // shards_of).reshape((-1,) + (1,) * (len(dims) - 1 - axis_at))
    return gain


def normal_values(own_key, extent, scale, reach, shards=(), kind=jnp.bfloat16):
    drawn = jax.random.normal(own_key, extent, jnp.float32) * scale
    if len(shards) > 0:
        drawn = block_scale(own_key, extent, shards, -0.22, 0.18) * drawn
    return jnp.clip(drawn, min=-reach, max=reach).astype(kind)


def setup_inputs(seed: int = 0) -> dict:
    key_of = jax.random.split(jax.random.key(seed), 6)
    return {
        "tokens": normal_values(key_of[0], (GROUPS, NDOCS, BLK, D), 1.0, 6.0, ((0, 4), (1, 64))),
        "lengths": draw_lengths(jax.random.fold_in(key_of[5], 71), 0),
        "queries": normal_values(key_of[2], (GROUPS, NDOCS, QW), 1.0, 6.0, ((0, 4), (1, 64))),
        "positives": draw_positives(jax.random.fold_in(key_of[5], 71), 0),
        "kv_weight": normal_values(key_of[4], (D, KVW), D ** -0.5, 0.09375, ((0, 4),)),
    }


SOFTMAX_TEMPER = 0.05

def group_pass(tokens, lengths, queries, positives, kv_weight):
    doc_total = tokens.shape[0]
    group_size = QH // KVH
    score_scale = HD ** (-0.5)
    flat_rows = tokens.reshape(doc_total * BLK, D)
    keyval = jnp.dot(flat_rows, kv_weight, preferred_element_type=jnp.float32).astype(jnp.bfloat16)
    keyval = keyval.reshape(doc_total, BLK, KVW)
    live = jnp.arange(BLK)[None, :] < lengths[:, None]
    query_heads = queries.astype(jnp.float32).reshape(doc_total, KVH, group_size, HD)
    key_heads = keyval[..., :KVH * HD].astype(jnp.float32).reshape(doc_total, BLK, KVH, HD)
    value_heads = keyval[..., KVH * HD:].astype(jnp.float32).reshape(doc_total, BLK, KVH, HD)
    scores = jnp.einsum('nkgd,nrkd->nkgr', query_heads, key_heads) * score_scale
    row_mask = live[:, None, None, :]
    expvals = jnp.where(row_mask, jnp.exp(jnp.where(row_mask, scores, 0.0)), 0.0)
    attn = expvals / lax.optimization_barrier(jnp.sum(expvals, axis=-1, keepdims=True))
    attn_b = lax.optimization_barrier(attn.astype(jnp.bfloat16)).astype(jnp.float32)
    readout = jnp.einsum('nkgr,nrkd->nkgd', attn_b, value_heads).reshape(doc_total, QW)
    length_norm = jnp.sqrt(lax.optimization_barrier(jnp.sum(readout * readout, axis=-1, keepdims=True)) + 1e-06)
    unit_vec = readout / length_norm
    embedding_vectors = unit_vec.astype(jnp.bfloat16)
    similarity_matrix = jnp.dot(embedding_vectors, embedding_vectors.T, preferred_element_type=jnp.float32) / SOFTMAX_TEMPER
    columns = jnp.arange(doc_total)
    self_pair = columns[:, None] == columns[None, :]
    sim_exp = jnp.where(self_pair, 0.0, jnp.exp(similarity_matrix))
    row_total = lax.optimization_barrier(jnp.sum(sim_exp, axis=-1))
    picked = positives[:, None] == columns[None, :]
    document_loss = jnp.log(row_total) - lax.optimization_barrier(jnp.sum(jnp.where(picked, similarity_matrix, 0.0), axis=-1))
    probability = (sim_exp / row_total[:, None]).astype(jnp.bfloat16)
    chosen_partner = picked.astype(jnp.bfloat16)
    gradient_unit_vector = (jnp.dot(probability, embedding_vectors, preferred_element_type=jnp.float32) + jnp.dot(probability.T, embedding_vectors, preferred_element_type=jnp.float32) - jnp.dot(chosen_partner, embedding_vectors, preferred_element_type=jnp.float32) - jnp.dot(chosen_partner.T, embedding_vectors, preferred_element_type=jnp.float32)) / SOFTMAX_TEMPER
    grad_read = (gradient_unit_vector - unit_vec * lax.optimization_barrier(jnp.sum(unit_vec * gradient_unit_vector, axis=-1, keepdims=True))) / length_norm
    grad_read = lax.optimization_barrier(grad_read.astype(jnp.bfloat16)).astype(jnp.float32)
    grad_heads = grad_read.reshape(doc_total, KVH, group_size, HD)
    grad_w = jnp.einsum('nkgd,nrkd->nkgr', grad_heads, value_heads)
    grad_score = attn * (grad_w - lax.optimization_barrier(jnp.sum(attn * grad_w, axis=-1, keepdims=True))) * score_scale
    grad_score = lax.optimization_barrier(grad_score.astype(jnp.bfloat16)).astype(jnp.float32)
    grad_query = jnp.einsum('nkgr,nrkd->nkgd', grad_score, key_heads).reshape(doc_total, QW)
    grad_key = jnp.einsum('nkgr,nkgd->nrkd', grad_score, query_heads).reshape(doc_total, BLK, KVH * HD)
    grad_value = jnp.einsum('nkgr,nkgd->nrkd', attn_b, grad_heads).reshape(doc_total, BLK, KVH * HD)
    grad_keyval = jnp.concatenate([grad_key, grad_value], axis=-1)
    grad_keyval = jnp.where(live[:, :, None], grad_keyval, 0.0).astype(jnp.bfloat16)
    flat_grad = grad_keyval.reshape(doc_total * BLK, KVW)
    grad_tok = jnp.dot(flat_grad, kv_weight.T, preferred_element_type=jnp.float32).astype(jnp.bfloat16)
    grad_w_part = jnp.dot(flat_rows.T, flat_grad, preferred_element_type=jnp.float32)
    return (document_loss, grad_tok.reshape(doc_total, BLK, D), grad_query.astype(jnp.bfloat16), grad_w_part)

def reference(tokens, lengths, queries, positives, kv_weight):
    losses = []
    token_grads = []
    query_grads = []
    weight_grad = jnp.zeros((D, KVW), jnp.float32)
    for group_index in range(GROUPS):
        loss_g, tok_g, query_g, weight_g = group_pass(tokens[group_index], lengths[group_index], queries[group_index], positives[group_index], kv_weight)
        losses.append(loss_g)
        token_grads.append(tok_g)
        query_grads.append(query_g)
        weight_grad = weight_grad + weight_g
    return (jnp.stack(losses), jnp.stack(token_grads), jnp.stack(query_grads), weight_grad)
```

```python
import jax
import jax.numpy as jnp
from jax import lax
from jax.sharding import PartitionSpec as P

QH = 14
KVH = 2
GRP = QH // KVH
HD = 128
QW = QH * HD
KVW = 2 * KVH * HD
HALF = QW // 2
TYPES = 2 * KVH

SOFTMAX_TEMPER = 0.05

NZ, NX, NC, NY = 8, 4, 2, 4
N_DP = NZ * NX * NC


def dp_index(z, x, c):
    return (z * NX + x) * NC + c


OTHER_CORE = [(i, i ^ 1) for i in range(N_DP)]
CHIPS = [[dp_index(z, x, c) for z in range(NZ) for x in range(NX)] for c in range(NC)]


def y_shift(k):
    return [(i, (i + k) % NY) for i in range(NY)]


def z_shift(k):
    return [
        (dp_index(z, x, c), dp_index((z + k) % NZ, x, c))
        for z in range(NZ)
        for x in range(NX)
        for c in range(NC)
    ]


OWNERS = [
    [
        dp_index(2 * t + p, x, c) * NY + y
        for p in range(2)
        for x in range(NX)
        for y in range(NY)
    ]
    for t in range(TYPES)
    for c in range(NC)
]


def pick_core(core, mine, other):
    return (jnp.where(core == 0, mine, other), jnp.where(core == 0, other, mine))


def gather_weight(kv_weight, core, y):
    rows = kv_weight.shape[0]
    half = lax.dynamic_slice(kv_weight, (0, core * (KVW // 2)), (rows, KVW // 2))
    got = [lax.ppermute(half, "fsdp", y_shift(k)) for k in (3, 2, 1)]
    mine = jnp.concatenate(got, axis=0)
    other = lax.ppermute(mine, "dp", OTHER_CORE)
    rest = jnp.concatenate(pick_core(core, mine, other), axis=1)
    ring = jnp.concatenate([kv_weight, rest, kv_weight, rest], axis=0)
    start = (NY - y) % NY
    return lax.dynamic_slice(ring, (start * rows, 0), (NY * rows, KVW))


def gather_docs(rows, core):
    docs = rows.shape[0]
    other = lax.ppermute(rows, "dp", OTHER_CORE)
    chip = jnp.concatenate(pick_core(core, rows, other), axis=0)
    width = chip.shape[1] // 2
    half = lax.dynamic_slice(chip, (0, core * width), (NC * docs, width))
    spread = jnp.broadcast_to(half[None], (NZ * NX, NC * docs, width))
    got = lax.all_to_all(spread, "dp", 0, 0, axis_index_groups=CHIPS)
    got = got.reshape(NZ * NX * NC * docs, width)
    return pick_core(core, got, lax.ppermute(got, "dp", OTHER_CORE))


def contrast(unit, norm, own_positives, core):
    docs = unit.shape[0]
    emb = unit.astype(jnp.bfloat16)
    mark = jnp.broadcast_to(own_positives.astype(jnp.bfloat16)[:, None], (docs, HD))
    packed = jnp.concatenate([emb[:, :HALF], mark, emb[:, HALF:], mark], axis=1)
    first, second = gather_docs(packed, core)
    everyone = jnp.concatenate([first[:, :HALF], second[:, :HALF]], axis=1)
    positives = first[:, HALF].astype(jnp.int32)
    total_docs = everyone.shape[0]
    sim = (
        lax.dot_general(
            everyone, everyone, (((1,), (1,)), ((), ())), preferred_element_type=jnp.float32
        )
        / SOFTMAX_TEMPER
    )
    ids = jnp.arange(total_docs)
    sim_exp = jnp.where(ids[:, None] == ids[None, :], 0.0, jnp.exp(sim))
    total = jnp.sum(sim_exp, axis=-1)
    picked = positives[:, None] == ids[None, :]
    loss = jnp.log(total) - jnp.sum(jnp.where(picked, sim, 0.0), axis=-1)
    prob = (sim_exp / total[:, None]).astype(jnp.bfloat16)
    pick = picked.astype(jnp.bfloat16)
    first_id = lax.axis_index("dp") * docs
    own = lambda a: lax.dynamic_slice_in_dim(a, first_id, docs, 0)
    coef = jnp.concatenate([own(prob), own(prob.T), own(pick), own(pick.T)], axis=0)
    parts = jnp.dot(coef, everyone, preferred_element_type=jnp.float32).reshape(4, docs, QW)
    grad_unit = (parts[0] + parts[1] - parts[2] - parts[3]) / SOFTMAX_TEMPER
    grad_read = (
        (grad_unit - unit * jnp.sum(unit * grad_unit, axis=-1, keepdims=True)) / norm
    ).astype(jnp.bfloat16)
    return own(loss), grad_read


def exchange_types(factors):
    z = lax.axis_index("dp") // (NX * NC)
    quad = z // 2
    take = lambda t: lax.dynamic_index_in_dim(factors, t, 0, keepdims=False)
    got = [take(quad)]
    for k in (1, 2, 3):
        got.append(lax.ppermute(take((quad + k) % TYPES), "dp", z_shift(2 * k)))
    return jnp.concatenate(got, axis=0)


def reduce_weight(factors, width, core):
    quads = exchange_types(factors)
    both = jnp.concatenate([quads, lax.ppermute(quads, "dp", OTHER_CORE)], axis=0)
    heads = both[:, width:].reshape(-1, 2, NX, NC, NY, HD // (2 * NX * NC * NY))
    heads = lax.dynamic_index_in_dim(heads, core, 3, keepdims=False)
    heads = heads.reshape(both.shape[0], HD // NC)
    part = lax.dot_general(
        heads, both[:, :width], (((0,), (0,)), ((), ())), preferred_element_type=jnp.float32
    ).astype(jnp.bfloat16)
    pieces = part.reshape(2 * NX * NY, -1, width)
    got = lax.all_to_all(pieces, ("dp", "fsdp"), 0, 0, axis_index_groups=OWNERS)
    return jnp.sum(got.astype(jnp.float32), axis=0).T


def local(tokens, lengths, queries, positives, kv_weight):
    own_tokens = tokens[0]
    docs, block, width = own_tokens.shape
    core = lax.axis_index("dp") % NC
    y = lax.axis_index("fsdp")
    weight = gather_weight(kv_weight, core, y)
    rows = own_tokens.reshape(-1, width)
    live = jnp.arange(block)[None, :] < lengths[0][:, None]
    mask = live[:, None, None, :]
    keyval = jnp.dot(rows, weight, preferred_element_type=jnp.float32).astype(jnp.bfloat16)
    keyval = keyval.reshape(docs, block, 2, KVH, HD)
    keys, values = keyval[:, :, 0], keyval[:, :, 1]
    heads = queries[0].reshape(docs, KVH, GRP, HD)
    scores = jnp.einsum("nkgd,nrkd->nkgr", heads, keys, preferred_element_type=jnp.float32)
    scores = scores * HD ** (-0.5)
    expvals = jnp.where(mask, jnp.exp(jnp.where(mask, scores, 0.0)), 0.0)
    attn = expvals / jnp.sum(expvals, axis=-1, keepdims=True)
    attn_b = attn.astype(jnp.bfloat16)
    readout = jnp.einsum("nkgr,nrkd->nkgd", attn_b, values, preferred_element_type=jnp.float32)
    readout = readout.reshape(docs, QW)
    norm = jnp.sqrt(jnp.sum(readout * readout, axis=-1, keepdims=True) + 1e-06)
    unit = readout / norm
    loss, grad_read = contrast(unit, norm, positives[0], core)
    grad_heads = grad_read.reshape(docs, KVH, GRP, HD)
    grad_w = jnp.einsum("nkgd,nrkd->nkgr", grad_heads, values, preferred_element_type=jnp.float32)
    grad_score = attn * (grad_w - jnp.sum(attn * grad_w, axis=-1, keepdims=True)) * HD ** (-0.5)
    grad_score = grad_score.astype(jnp.bfloat16)
    grad_query = jnp.einsum("nkgr,nrkd->nkgd", grad_score, keys, preferred_element_type=jnp.float32)
    grad_query = grad_query.reshape(docs, QW).astype(jnp.bfloat16)

    mix = jnp.stack([grad_score, attn_b], axis=1)
    right = jnp.stack([heads, grad_heads], axis=1)
    left = jnp.einsum("ntkgr,nrw->tkngw", mix, own_tokens, preferred_element_type=jnp.float32)
    factors = jnp.concatenate(
        [left.astype(jnp.bfloat16), right.transpose(1, 2, 0, 3, 4)], axis=-1
    ).reshape(TYPES, docs * GRP, width + HD)
    factors = jnp.pad(factors, ((0, 0), (0, 2), (0, 0)))
    grad_weight = reduce_weight(factors, width, core)

    grad_keyval = jnp.einsum(
        "ntkgr,ntkgd->nrtkd", mix, right, preferred_element_type=jnp.float32
    ).astype(jnp.bfloat16)
    grad_tok = lax.dot_general(
        grad_keyval.reshape(docs * block, KVW),
        weight,
        (((1,), (1,)), ((), ())),
        preferred_element_type=jnp.float32,
    ).astype(jnp.bfloat16)
    grad_tok = grad_tok.reshape(docs, block, width)
    return (loss[None], grad_tok[None], grad_query[None], grad_weight)


def solution(mesh):
    placed = (
        P("fsdp", "dp", None, None),
        P("fsdp", "dp"),
        P("fsdp", "dp", None),
        P("fsdp", "dp"),
        P("fsdp", None),
    )
    return jax.shard_map(
        local,
        mesh=mesh,
        in_specs=placed,
        out_specs=(
            P("fsdp", "dp"),
            P("fsdp", "dp", None, None),
            P("fsdp", "dp", None),
            P(None, ("dp", "fsdp")),
        ),
        check_vma=False,
    )
```

```python
import jax
import jax.numpy as jnp
from jax import lax
from jax.experimental import pallas as pl
from jax.experimental.pallas import tpu as pltpu
from jax.sharding import PartitionSpec as P

QH = 14
KVH = 2
GRP = QH // KVH
SLOT = 8
HD = 128
QW = QH * HD
KVW = 2 * KVH * HD
HALF = QW // 2
TYPES = 2 * KVH
DOCS = 2
SIDE = DOCS * SLOT
ROWS = KVH * SIDE
SOFTMAX_TEMPER = 0.05

NZ, NX, NC, NY = 8, 4, 2, 4
N_DP = NZ * NX * NC

F32 = jnp.float32
BF16 = jnp.bfloat16


def dp_index(z, x, c):
    return (z * NX + x) * NC + c


OTHER_CORE = [(i, i ^ 1) for i in range(N_DP)]
X_MATE = [(i, i ^ NC) for i in range(N_DP)]


Y_ACROSS = [(i, (i + 2) % NY) for i in range(NY)]


def y_mirror():
    return [
        (dp * NY + y, dp * NY + (y + (1 if dp % NC else NY - 1)) % NY)
        for dp in range(N_DP)
        for y in range(NY)
    ]


def plane_shift(dz=0, dx=0, mirror=False):
    pairs = []
    for z in range(NZ):
        for x in range(NX):
            for c in range(NC):
                sign = -1 if mirror and c == 0 else 1
                to = dp_index((z + sign * dz) % NZ, (x + sign * dx) % NX, c)
                pairs.append((dp_index(z, x, c), to))
    return pairs


OWNERS = [
    [
        dp_index(2 * t + p, x, c) * NY + y
        for p in range(2)
        for x in range(NX)
        for y in range(NY)
    ]
    for t in range(TYPES)
    for c in range(NC)
]


def parity_shift(k):
    pairs = []
    for z in range(NZ):
        to = (z + (k if z % 2 == 0 else -k)) % NZ
        pairs += [(dp_index(z, x, c), dp_index(to, x, c)) for x in range(NX) for c in range(NC)]
    return pairs


def dot_nn(a, b):
    return jnp.dot(a, b, preferred_element_type=F32)


def tie(a, *after):
    return lax.optimization_barrier((a, *after))[0]


def dot_tn(a, b):
    return lax.dot_general(a, b, (((0,), (0,)), ((), ())), preferred_element_type=F32)


def dot_nt(a, b):
    return lax.dot_general(a, b, (((1,), (1,)), ((), ())), preferred_element_type=F32)


def call(body, scalars, arrays, outs, scratch=(), flops=0):
    smem = [pl.BlockSpec(memory_space=pltpu.SMEM)] * len(scalars)
    vmem = [pl.BlockSpec(memory_space=pltpu.VMEM)] * len(arrays)
    return pl.pallas_call(
        body,
        out_shape=[jax.ShapeDtypeStruct(s, d) for s, d in outs],
        in_specs=smem + vmem,
        out_specs=[pl.BlockSpec(memory_space=pltpu.VMEM)] * len(outs),
        scratch_shapes=list(scratch),
        compiler_params=pltpu.CompilerParams(vmem_limit_bytes=20 * 1024 * 1024),
        cost_estimate=pl.CostEstimate(flops=flops, bytes_accessed=0, transcendentals=0),
    )(*scalars, *arrays)


def row_mask(lens, block):
    rows = lax.broadcasted_iota(jnp.int32, (ROWS, DOCS * block), 0)
    cols = lax.broadcasted_iota(jnp.int32, (ROWS, DOCS * block), 1)
    row_doc = (rows // SLOT) % DOCS
    length = jnp.where(row_doc == 0, lens[0], lens[1])
    at = cols - row_doc * block
    return (at >= 0) & (at < length)


def block_at(place, k, shard):
    return pl.multiple_of(lax.rem(place[0] + k, NY) * shard, shard)


def near_at(place, shard):
    return block_at(place, jnp.where(place[1] == 0, 1, NY - 1), shard)


def near_other_at(place, shard):
    return block_at(place, jnp.where(place[1] == 0, NY - 1, 1), shard)


def across_block(place, mine, mate, other, other_mate):
    low, first = place[3] == 0, place[1] == 0
    a = [jnp.where(low, mine[...], mate[...]), jnp.where(low, mate[...], mine[...])]
    b = [jnp.where(low, other[...], other_mate[...]), jnp.where(low, other_mate[...], other[...])]
    keys = [jnp.where(first, p, q) for p, q in zip(a, b)]
    values = [jnp.where(first, q, p) for p, q in zip(a, b)]
    return jnp.concatenate(keys + values, axis=1)


def own_body(place, tokens, weight, queries, out, rows, flat):
    shard = weight.shape[0]
    out[...] = dot_nn(tokens[:, pl.ds(block_at(place, 0, shard), shard)], weight[...])
    from_lanes(queries[...].astype(F32), flat)
    rows[...] = flat[...].astype(BF16)


def near_body(place, tokens, weight, before, out):
    shard = weight.shape[0]
    part = dot_nn(tokens[:, pl.ds(near_at(place, shard), shard)], weight[...])
    out[...] = before[...] + part


def from_lanes(a, out):
    out[...] = jnp.zeros_like(out)
    for kvh in range(KVH):
        for doc in range(DOCS):
            for g in range(GRP):
                i = kvh * GRP + g
                r = kvh * SIDE + doc * SLOT + g
                out[r : r + 1, :] = a[doc : doc + 1, i * HD : (i + 1) * HD]


def to_lanes(rows, kvh, out):
    for doc in range(DOCS):
        for g in range(GRP):
            head = kvh * GRP + g
            r = doc * SLOT + g
            out[doc : doc + 1, head * HD : (head + 1) * HD] = rows[r : r + 1]


def head(a, i):
    return a[:, i * HD : (i + 1) * HD]


def attend_body(
    place, lens, marks, tokens, before, near_other, w0, w1, w2, w3, queries,
    keyval, attn, packed, unit, norm, flat,
):
    shard = near_other.shape[0]
    blocks = [
        (near_other_at(place, shard), near_other[...]),
        (block_at(place, 2, shard), across_block(place, w0, w1, w2, w3)),
    ]
    total = before[...]
    for at, block in blocks:
        total += dot_nn(tokens[:, pl.ds(at, shard)], block)
    both = total.astype(BF16)
    keyval[...] = both
    scores = jnp.concatenate(
        [dot_nt(queries[h * SIDE : (h + 1) * SIDE, :], head(both, h)) for h in range(KVH)], axis=0
    ) * HD ** (-0.5)
    mask = row_mask(lens, both.shape[0] // DOCS)
    expvals = jnp.where(mask, jnp.exp(jnp.where(mask, scores, 0.0)), 0.0)
    probs = expvals / jnp.sum(expvals, axis=-1, keepdims=True)
    attn[...] = probs
    probs = probs.astype(BF16)
    flat[...] = jnp.zeros_like(flat)
    for h in range(KVH):
        to_lanes(dot_nn(probs[h * SIDE : (h + 1) * SIDE], head(both, KVH + h)), h, flat)
    readout = flat[...]
    length = jnp.sqrt(jnp.sum(readout * readout, axis=-1, keepdims=True) + 1e-06)
    vec = readout / length
    unit[...] = vec
    norm[...] = jnp.broadcast_to(length, norm.shape)
    emb = vec.astype(BF16)
    doc_at = lax.broadcasted_iota(jnp.int32, (SLOT, HD), 0)
    mark = jnp.where(doc_at == 0, marks[0], marks[1]).astype(F32).astype(BF16)
    whole = jnp.concatenate([emb[:, :HALF], mark, emb[:, HALF:], mark], axis=1)
    packed[...] = whole[:DOCS]


def mix_body(tokens, attn, mixed):
    mixed[...] = dot_nn(attn[...].astype(BF16), tokens[...]).astype(BF16)


def backward_body(
    place, tokens, attn, mixed, queries, keyval, unit, norm,
    ring, e0, e1, e2, e3, f0, f1, f2, f3,
    loss, grad_score, grad_rows, grad_query, factors, flat, lanes,
):
    first = place[1] == 0
    gathered = join_docs(first, ring, (e0, e1, e2, e3), (f0, f1, f2, f3))
    span = HALF + HD
    everyone = jnp.concatenate([gathered[:, :HALF], gathered[:, span : span + HALF]], axis=1)
    total_docs = everyone.shape[0]
    marks = gathered[:, HALF:span].astype(F32)
    ids = lax.broadcasted_iota(jnp.int32, (total_docs, total_docs), 0)
    cols = lax.broadcasted_iota(jnp.int32, (total_docs, total_docs), 1)
    sim = dot_nt(everyone, everyone) / SOFTMAX_TEMPER
    sim_exp = jnp.where(ids == cols, 0.0, jnp.exp(sim))
    total = jnp.sum(sim_exp, axis=-1, keepdims=True)
    picked = marks == doc_ids(place, cols).astype(F32)
    all_loss = jnp.log(total) - jnp.sum(jnp.where(picked, sim, 0.0), axis=-1, keepdims=True)
    prob = (sim_exp / total).astype(BF16)
    pick = jnp.where(picked, 1.0, 0.0).astype(BF16)
    at = place[1] * DOCS
    slots = lax.broadcasted_iota(jnp.int32, (SLOT, total_docs), 0)
    here = lax.broadcasted_iota(jnp.int32, (SLOT, total_docs), 1)
    chosen = (here == at + slots) & (slots < DOCS)
    own_rows = jnp.where(chosen, 1.0, 0.0).astype(BF16)
    lane = lax.broadcasted_iota(jnp.int32, (total_docs, HD), 0)
    slot = lax.broadcasted_iota(jnp.int32, (total_docs, HD), 1)
    loss[...] = jnp.sum(jnp.where(lane == at + slot, all_loss, 0.0), axis=0, keepdims=True)
    coef = jnp.concatenate(
        [
            dot_nn(own_rows, prob),
            dot_nt(own_rows, prob),
            dot_nn(own_rows, pick),
            dot_nt(own_rows, pick),
        ],
        axis=0,
    ).astype(BF16)
    parts = dot_nn(coef, everyone)
    grad_unit = (parts[:8] + parts[8:16] - parts[16:24] - parts[24:]) / SOFTMAX_TEMPER
    vec = unit[...]
    along = jnp.sum(vec * grad_unit, axis=-1, keepdims=True)
    grad_read = (grad_unit - vec * along) / norm[:, :1]
    from_lanes(grad_read, flat)
    heads = flat[...].astype(BF16)
    grad_rows[...] = heads
    sides = [slice(h * SIDE, (h + 1) * SIDE) for h in range(KVH)]
    grad_w = jnp.concatenate(
        [dot_nt(heads[sides[h]], head(keyval, KVH + h)) for h in range(KVH)], axis=0
    )
    probs = attn[...]
    inner = jnp.sum(probs * grad_w, axis=-1, keepdims=True)
    score = (probs * (grad_w - inner) * HD ** (-0.5)).astype(BF16)
    grad_score[...] = score
    for h in range(KVH):
        to_lanes(dot_nn(score[sides[h]], head(keyval, h)), h, lanes)
    grad_query[...] = lanes[:DOCS, :].astype(BF16)
    wide = GRP * HD
    slot_rows = lax.broadcasted_iota(jnp.int32, (SIDE, wide), 0)
    halves = [dot_nn(score, tokens[...]), mixed[...].astype(F32)]
    tails = [queries[...].astype(F32), grad_read]
    for kind in range(2):
        for h in range(KVH):
            tail = tails[kind][:, h * wide : (h + 1) * wide]
            tail = jnp.where(slot_rows < SLOT, tail[0:1], tail[1:2])
            part = halves[kind][sides[h]]
            joined = jnp.where(slot_rows % SLOT == GRP, tail, part[:, :wide])
            factors[kind * KVH + h, :, :wide] = joined.astype(BF16)
            factors[kind * KVH + h, :, wide:] = part[:, wide:].astype(BF16)


def token_body(
    place, grad_score, attn, query_rows, grad_rows, own, near, near_other, w0, w1, w2, w3, out, done
):
    shard = own.shape[0]
    probs = attn[...].astype(BF16)
    sides = [slice(h * SIDE, (h + 1) * SIDE) for h in range(KVH)]
    parts = [dot_tn(grad_score[s, :], query_rows[s, :]) for s in sides]
    parts += [dot_tn(probs[s], grad_rows[s, :]) for s in sides]
    grad_keyval = jnp.concatenate(parts, axis=1).astype(BF16)
    blocks = [
        (block_at(place, 0, shard), own[...]),
        (near_at(place, shard), near[...]),
        (near_other_at(place, shard), near_other[...]),
        (block_at(place, 2, shard), across_block(place, w0, w1, w2, w3)),
    ]
    for at, block in blocks:
        out[:, pl.ds(at, shard)] = dot_nt(grad_keyval, block).astype(BF16)
    done[...] = probs[:SLOT, :HD].astype(F32)


def chip_body(place, mine, other, chip, half):
    first = place[1] == 0
    a, b = mine[...].astype(F32), other[...].astype(F32)
    whole = jnp.concatenate([jnp.where(first, a, b), jnp.where(first, b, a)], axis=0).astype(BF16)
    chip[...] = whole
    width = half.shape[1]
    half[...] = jnp.where(first, whole[:, :width], whole[:, width:])


def ring_body(place, chip, near, far, near_other, far_other, ring, half):
    first = place[1] == 0
    a, b = near[...].astype(F32), near_other[...].astype(F32)
    c, d = far[...].astype(F32), far_other[...].astype(F32)
    plus, minus = jnp.where(first, a, b), jnp.where(first, b, a)
    across = jnp.concatenate([jnp.where(first, c, d), jnp.where(first, d, c)], axis=1)
    whole = jnp.concatenate([chip[...].astype(F32), plus, across, minus], axis=0).astype(BF16)
    ring[...] = whole
    width = half.shape[1]
    half[...] = jnp.where(first, whole[:, :width], whole[:, width:])


def gather_docs(packed, place, before_ring):
    docs, wide = packed.shape
    swap = lambda a: lax.ppermute(a, "dp", OTHER_CORE)
    count = NC * docs
    chip, half = call(
        chip_body, (place,), (packed, swap(packed)),
        [((count, wide), BF16), ((count, wide // 2), BF16)],
    )
    near = lax.ppermute(chip, "dp", plane_shift(dx=1, mirror=True))
    far = lax.ppermute(half, "dp", plane_shift(dx=2))
    far = tie(far, before_ring)
    count *= NX
    ring, half = call(
        ring_body, (place,), (chip, near, far, swap(near), swap(far)),
        [((count, wide), BF16), ((count, wide // 2), BF16)],
    )
    blocks = [lax.ppermute(ring, "dp", plane_shift(dz=k, mirror=True)) for k in (1, 2, 3)]
    blocks.append(lax.ppermute(half, "dp", plane_shift(dz=4)))
    return (ring, *blocks, *[swap(a) for a in blocks])


def join_docs(first, ring, blocks, others):
    pairs = [(a[...], b[...]) for a, b in zip(blocks, others)]
    plus = [jnp.where(first, a, b) for a, b in pairs]
    minus = [jnp.where(first, b, a) for a, b in pairs]
    across = jnp.concatenate([plus[3], minus[3]], axis=1)
    return jnp.concatenate(
        [ring[...], plus[0], plus[1], plus[2], across, minus[2], minus[1], minus[0]], axis=0
    )


def doc_ids(place, slots):
    dp = place[2] // DOCS
    z, x = dp // (NX * NC), (dp // NC) % NX
    count = NC * DOCS
    at_z = (z + slots // (NX * count)) % NZ
    at_x = (x + (slots // count) % NX) % NX
    return (at_z * NX + at_x) * count + slots % count


def outer_body(place, a0, a1, a2, a3, b0, b1, b2, b3, out):
    rows = jnp.concatenate([a[...] for a in (a0, a1, a2, a3, b0, b1, b2, b3)], axis=0)
    count = rows.shape[0]
    to = lax.broadcasted_iota(jnp.int32, (count, count), 0)
    at = lax.broadcasted_iota(jnp.int32, (count, count), 1)
    spread = jnp.where(at == (to // SLOT) * SLOT + GRP, 1.0, 0.0).astype(BF16)
    tails = dot_nn(spread, rows[:, : GRP * HD])
    slot = lax.broadcasted_iota(jnp.int32, (count, HD), 0) % SLOT
    heads = jnp.zeros((count, HD), F32)
    for g in range(GRP):
        heads = jnp.where(slot == g, tails[:, g * HD : (g + 1) * HD], heads)
    slots = lax.broadcasted_iota(jnp.int32, (HD // NC, HD), 0)
    cols = lax.broadcasted_iota(jnp.int32, (HD // NC, HD), 1)
    cell = HD // (2 * NX * NC)
    chosen = cols == ((slots // cell) * NC + place[1]) * cell + slots % cell
    chosen = jnp.where(chosen, 1.0, 0.0).astype(BF16)
    left = dot_nt(chosen, heads.astype(BF16)).astype(BF16)
    out[...] = dot_nn(left, rows).astype(BF16)


def exchange_types(factors):
    z = lax.axis_index("dp") // (NX * NC)
    sign = 1 - 2 * (z % 2)
    take = lambda to: lax.dynamic_index_in_dim(factors, (to % NZ) // 2, 0, keepdims=False)
    quads = [take(z)]
    for k in (-1, -3, 2):
        quads.append(lax.ppermute(take(z + NZ + sign * k), "dp", parity_shift(k)))
    return quads


def reduce_weight(quads, place):
    swapped = [lax.ppermute(a, "dp", OTHER_CORE) for a in quads]
    width = quads[0].shape[1]
    (part,) = call(outer_body, (place,), (*quads, *swapped), [((HD // NC, width), BF16)])
    pieces = part.reshape(2 * NX * NY, -1, width)
    got = lax.all_to_all(pieces, ("dp", "fsdp"), 0, 0, axis_index_groups=OWNERS)
    return jnp.sum(got.astype(F32), axis=0).T


def local(tokens, lengths, queries, positives, kv_weight):
    docs, block, width = tokens.shape[1:]
    shard = kv_weight.shape[0]
    count = docs * block
    dp = lax.axis_index("dp")
    core = dp % NC
    parity = (dp // NC) % 2
    y = lax.axis_index("fsdp")
    place = jnp.stack([y, core, dp * docs, parity]).astype(jnp.int32)
    rows = tokens.reshape(count, width)
    swap = lambda a: lax.ppermute(a, "dp", OTHER_CORE)

    piece = lax.dynamic_slice(kv_weight, (0, (2 * core + parity) * HD), (shard, HD))
    mine = lax.ppermute(piece, "fsdp", Y_ACROSS)
    near = lax.ppermute(kv_weight, ("dp", "fsdp"), y_mirror())
    mate = lax.ppermute(mine, "dp", X_MATE)

    flops = 2 * count * shard * KVW
    part, query_rows = call(
        own_body, (place,), (rows, kv_weight, queries[0]),
        [((count, KVW), F32), ((ROWS, HD), BF16)], [pltpu.VMEM((ROWS, HD), F32)], flops=flops,
    )
    near = tie(near, mate, part)
    across = (mine, mate, swap(mine), swap(mate))
    near_other = swap(near)
    (part,) = call(near_body, (place,), (rows, near, part), [((count, KVW), F32)], flops=flops)
    keyval, attn, packed, unit, norm = call(
        attend_body,
        (place, lengths[0], positives[0]),
        (rows, part, near_other, *across, query_rows),
        [
            ((count, KVW), BF16),
            ((ROWS, count), F32),
            ((docs, 2 * (HALF + HD)), BF16),
            ((SLOT, QW), F32),
            ((SLOT, HD), F32),
        ],
        [pltpu.VMEM((SLOT, QW), F32)],
        flops=2 * flops,
    )
    (mixed,) = call(
        mix_body, (), (rows, attn), [((ROWS, width), BF16)], flops=2 * ROWS * width * count
    )
    everyone = gather_docs(packed, place, mixed)
    loss, grad_score, grad_rows, grad_query, factors = call(
        backward_body,
        (place,),
        (rows, attn, mixed, queries[0], keyval, unit, norm, *everyone),
        [
            ((1, HD), F32),
            ((ROWS, count), BF16),
            ((ROWS, HD), BF16),
            ((docs, QW), BF16),
            ((TYPES, SIDE, width), BF16),
        ],
        [pltpu.VMEM((ROWS, HD), F32), pltpu.VMEM((SLOT, QW), F32)],
        flops=2 * ROWS * width * count,
    )
    quads = exchange_types(factors)
    grad_tok, done = call(
        token_body,
        (place,),
        (grad_score, attn, query_rows, grad_rows, kv_weight, near, near_other, *across),
        [((count, width), BF16), ((SLOT, HD), F32)],
        flops=4 * flops,
    )
    quads = [quads[0], *[tie(a, done) for a in quads[1:]]]
    grad_weight = reduce_weight(quads, place)
    return (loss[:, :docs], grad_tok.reshape(tokens.shape), grad_query[None], grad_weight)


def solution(mesh):
    placed = (
        P("fsdp", "dp", None, None),
        P("fsdp", "dp"),
        P("fsdp", "dp", None),
        P("fsdp", "dp"),
        P("fsdp", None),
    )
    return jax.shard_map(
        local,
        mesh=mesh,
        in_specs=placed,
        out_specs=(
            P("fsdp", "dp"),
            P("fsdp", "dp", None, None),
            P("fsdp", "dp", None),
            P(None, ("dp", "fsdp")),
        ),
        check_vma=False,
    )
```

```python
import jax
import jax.numpy as jnp
from jax import lax
from jax.experimental import pallas as pl
from jax.experimental.pallas import tpu as pltpu
from jax.sharding import PartitionSpec as P

QH = 14
KVH = 2
GRP = QH // KVH
SLOT = 8
HD = 128
QW = QH * HD
KVW = 2 * KVH * HD
HALF = QW // 2
TYPES = 2 * KVH
DOCS = 2
SIDE = DOCS * SLOT
ROWS = KVH * SIDE
FOLD = 4
ROUNDS = (0, -1, -3, 2)
SOFTMAX_TEMPER = 0.05

NZ, NX, NC, NY = 8, 4, 2, 4
N_DP = NZ * NX * NC

F32 = jnp.float32
BF16 = jnp.bfloat16


def dp_index(z, x, c):
    return (z * NX + x) * NC + c


OTHER_CORE = [(i, i ^ 1) for i in range(N_DP)]
CHIPS = [[dp_index(z, x, c) for z in range(NZ) for x in range(NX)] for c in range(NC)]
X_MATE = [(i, i ^ NC) for i in range(N_DP)]


Y_ACROSS = [(i, (i + 2) % NY) for i in range(NY)]


def y_mirror():
    return [
        (dp * NY + y, dp * NY + (y + (1 if dp % NC else NY - 1)) % NY)
        for dp in range(N_DP)
        for y in range(NY)
    ]


def plane_shift(dz=0, dx=0, mirror=False):
    pairs = []
    for z in range(NZ):
        for x in range(NX):
            for c in range(NC):
                sign = -1 if mirror and c == 0 else 1
                to = dp_index((z + sign * dz) % NZ, (x + sign * dx) % NX, c)
                pairs.append((dp_index(z, x, c), to))
    return pairs


OWNERS = [
    [
        dp_index(2 * t + p, x, c) * NY + y
        for p in range(2)
        for x in range(NX)
        for y in range(NY)
    ]
    for t in range(TYPES)
    for c in range(NC)
]


def parity_shift(k):
    pairs = []
    for z in range(NZ):
        to = (z + (k if z % 2 == 0 else -k)) % NZ
        pairs += [(dp_index(z, x, c), dp_index(to, x, c)) for x in range(NX) for c in range(NC)]
    return pairs


def dot_nn(a, b):
    return jnp.dot(a, b, preferred_element_type=F32)


def tie(a, *after):
    return lax.optimization_barrier((a, *after))[0]


def dot_tn(a, b):
    return lax.dot_general(a, b, (((0,), (0,)), ((), ())), preferred_element_type=F32)


def dot_nt(a, b):
    return lax.dot_general(a, b, (((1,), (1,)), ((), ())), preferred_element_type=F32)


def call(body, scalars, arrays, outs, scratch=(), flops=0, limit=4):
    smem = [pl.BlockSpec(memory_space=pltpu.SMEM)] * len(scalars)
    vmem = [pl.BlockSpec(memory_space=pltpu.VMEM)] * len(arrays)
    return pl.pallas_call(
        body,
        out_shape=[jax.ShapeDtypeStruct(s, d) for s, d in outs],
        in_specs=smem + vmem,
        out_specs=[pl.BlockSpec(memory_space=pltpu.VMEM)] * len(outs),
        scratch_shapes=list(scratch),
        compiler_params=pltpu.CompilerParams(vmem_limit_bytes=limit * 1024 * 1024),
        cost_estimate=pl.CostEstimate(flops=flops, bytes_accessed=0, transcendentals=0),
    )(*scalars, *arrays)


def row_mask(lens, block):
    rows = lax.broadcasted_iota(jnp.int32, (ROWS, DOCS * block), 0)
    cols = lax.broadcasted_iota(jnp.int32, (ROWS, DOCS * block), 1)
    row_doc = (rows // SLOT) % DOCS
    length = jnp.where(row_doc == 0, lens[0], lens[1])
    at = cols - row_doc * block
    return (at >= 0) & (at < length)


def block_at(place, k, shard):
    return pl.multiple_of(lax.rem(place[0] + k, NY) * shard, shard)


def near_at(place, shard):
    return block_at(place, jnp.where(place[1] == 0, 1, NY - 1), shard)


def near_other_at(place, shard):
    return block_at(place, jnp.where(place[1] == 0, NY - 1, 1), shard)


def across_block(place, mine, mate, other, other_mate):
    low, first = place[3] == 0, place[1] == 0
    a = [jnp.where(low, mine[...], mate[...]), jnp.where(low, mate[...], mine[...])]
    b = [jnp.where(low, other[...], other_mate[...]), jnp.where(low, other_mate[...], other[...])]
    keys = [jnp.where(first, p, q) for p, q in zip(a, b)]
    values = [jnp.where(first, q, p) for p, q in zip(a, b)]
    return jnp.concatenate(keys + values, axis=1)


def own_body(place, tokens, weight, queries, out, rows, flat):
    shard = weight.shape[0]
    out[...] = dot_nn(tokens[:, pl.ds(block_at(place, 0, shard), shard)], weight[...])
    from_lanes(queries[...].astype(F32), flat)
    rows[...] = flat[...].astype(BF16)


def near_body(place, tokens, weight, before, out):
    shard = weight.shape[0]
    part = dot_nn(tokens[:, pl.ds(near_at(place, shard), shard)], weight[...])
    out[...] = before[...] + part


def from_lanes(a, out):
    out[...] = jnp.zeros_like(out)
    for kvh in range(KVH):
        for doc in range(DOCS):
            for g in range(GRP):
                i = kvh * GRP + g
                r = kvh * SIDE + doc * SLOT + g
                out[r : r + 1, :] = a[doc : doc + 1, i * HD : (i + 1) * HD]


def to_lanes(rows, kvh, out):
    for doc in range(DOCS):
        for g in range(GRP):
            head = kvh * GRP + g
            r = doc * SLOT + g
            out[doc : doc + 1, head * HD : (head + 1) * HD] = rows[r : r + 1]


def head(a, i):
    return a[:, i * HD : (i + 1) * HD]


def attend_body(
    place, lens, marks, tokens, before, near_other, w0, w1, w2, w3, queries,
    keyval, attn, spread, unit, norm, flat,
):
    shard = near_other.shape[0]
    blocks = [
        (near_other_at(place, shard), near_other[...]),
        (block_at(place, 2, shard), across_block(place, w0, w1, w2, w3)),
    ]
    total = before[...]
    for at, block in blocks:
        total += dot_nn(tokens[:, pl.ds(at, shard)], block)
    both = total.astype(BF16)
    keyval[...] = both
    scores = jnp.concatenate(
        [dot_nt(queries[h * SIDE : (h + 1) * SIDE, :], head(both, h)) for h in range(KVH)], axis=0
    ) * HD ** (-0.5)
    mask = row_mask(lens, both.shape[0] // DOCS)
    expvals = jnp.where(mask, jnp.exp(jnp.where(mask, scores, 0.0)), 0.0)
    probs = expvals / jnp.sum(expvals, axis=-1, keepdims=True)
    attn[...] = probs
    probs = probs.astype(BF16)
    flat[...] = jnp.zeros_like(flat)
    for h in range(KVH):
        to_lanes(dot_nn(probs[h * SIDE : (h + 1) * SIDE], head(both, KVH + h)), h, flat)
    readout = flat[...]
    length = jnp.sqrt(jnp.sum(readout * readout, axis=-1, keepdims=True) + 1e-06)
    vec = readout / length
    unit[...] = vec
    norm[...] = jnp.broadcast_to(length, norm.shape)
    doc_at = lax.broadcasted_iota(jnp.int32, (SLOT, HD), 0)
    mark = jnp.where(doc_at == 0, marks[0], marks[1]).astype(F32)
    whole = jnp.concatenate([vec[:, :HALF], mark, vec[:, HALF:], mark], axis=1)
    wide = spread.shape[2]
    parts = [whole[:DOCS, i * wide : (i + 1) * wide] for i in range(FOLD)]
    folded = jnp.concatenate(parts, axis=0).astype(BF16)
    spread[...] = jnp.broadcast_to(folded[None], spread.shape)


def doc_ids(place, slots, half_docs):
    core = jnp.where(slots < half_docs, place[1], 1 - place[1])
    own = slots % half_docs
    return (own // DOCS) * (NC * DOCS) + core * DOCS + own % DOCS


def contrast_body(
    place, attn, keyval, unit, norm, mine, other,
    loss, grad_score, grad_rows, grad_query, grad_read, flat, lanes,
):
    half_docs = mine.shape[0] // FOLD
    total_docs = NC * half_docs
    to = lax.broadcasted_iota(jnp.int32, (half_docs, mine.shape[0]), 0)
    at = lax.broadcasted_iota(jnp.int32, (half_docs, mine.shape[0]), 1)
    base = (to // DOCS) * (FOLD * DOCS) + to % DOCS
    ones = [jnp.where(at == base + i * DOCS, 1.0, 0.0).astype(BF16) for i in range(FOLD)]
    unfold = lambda a: jnp.concatenate([dot_nn(one, a[...]) for one in ones], axis=1)
    gathered = jnp.concatenate([unfold(mine), unfold(other)], axis=0)
    span = HALF + HD
    everyone = jnp.concatenate([gathered[:, :HALF], gathered[:, span : span + HALF]], axis=1)
    everyone = everyone.astype(BF16)
    marks = gathered[:, HALF:span]
    ids = lax.broadcasted_iota(jnp.int32, (total_docs, total_docs), 0)
    cols = lax.broadcasted_iota(jnp.int32, (total_docs, total_docs), 1)
    sim = dot_nt(everyone, everyone) / SOFTMAX_TEMPER
    sim_exp = jnp.where(ids == cols, 0.0, jnp.exp(sim))
    total = jnp.sum(sim_exp, axis=-1, keepdims=True)
    picked = marks == doc_ids(place, cols, half_docs).astype(F32)
    all_loss = jnp.log(total) - jnp.sum(jnp.where(picked, sim, 0.0), axis=-1, keepdims=True)
    prob = (sim_exp / total).astype(BF16)
    pick = jnp.where(picked, 1.0, 0.0).astype(BF16)
    at = (place[2] // (NC * DOCS)) * DOCS
    slots = lax.broadcasted_iota(jnp.int32, (SLOT, total_docs), 0)
    here = lax.broadcasted_iota(jnp.int32, (SLOT, total_docs), 1)
    chosen = (here == at + slots) & (slots < DOCS)
    own_rows = jnp.where(chosen, 1.0, 0.0).astype(BF16)
    lane = lax.broadcasted_iota(jnp.int32, (total_docs, HD), 0)
    slot = lax.broadcasted_iota(jnp.int32, (total_docs, HD), 1)
    loss[...] = jnp.sum(jnp.where(lane == at + slot, all_loss, 0.0), axis=0, keepdims=True)
    coef = jnp.concatenate(
        [
            dot_nn(own_rows, prob),
            dot_nt(own_rows, prob),
            dot_nn(own_rows, pick),
            dot_nt(own_rows, pick),
        ],
        axis=0,
    ).astype(BF16)
    parts = dot_nn(coef, everyone)
    grad_unit = (parts[:8] + parts[8:16] - parts[16:24] - parts[24:]) / SOFTMAX_TEMPER
    vec = unit[...]
    along = jnp.sum(vec * grad_unit, axis=-1, keepdims=True)
    full = (grad_unit - vec * along) / norm[:, :1]
    grad_read[...] = full
    from_lanes(full, flat)
    heads = flat[...].astype(BF16)
    grad_rows[...] = heads
    sides = [slice(h * SIDE, (h + 1) * SIDE) for h in range(KVH)]
    grad_w = jnp.concatenate(
        [dot_nt(heads[sides[h]], head(keyval, KVH + h)) for h in range(KVH)], axis=0
    )
    probs = attn[...]
    inner = jnp.sum(probs * grad_w, axis=-1, keepdims=True)
    score = (probs * (grad_w - inner) * HD ** (-0.5)).astype(BF16)
    grad_score[...] = score
    for h in range(KVH):
        to_lanes(dot_nn(score[sides[h]], head(keyval, h)), h, lanes)
    grad_query[...] = lanes[:DOCS, :].astype(BF16)


def factor_body(place, tokens, grad_score, attn, queries, grad_read, *outs):
    sides = [slice(h * SIDE, (h + 1) * SIDE) for h in range(KVH)]
    wide = GRP * HD
    slot_rows = lax.broadcasted_iota(jnp.int32, (SIDE, wide), 0)
    both = jnp.concatenate([grad_score[...], attn[...].astype(BF16)], axis=0)
    mixed = dot_nn(both, tokens[...])
    tails = [queries[...].astype(F32), grad_read[...]]
    kinds = []
    for kind in range(2):
        for h in range(KVH):
            tail = tails[kind][:, h * wide : (h + 1) * wide]
            tail = jnp.where(slot_rows < SLOT, tail[0:1], tail[1:2])
            part = mixed[kind * ROWS : (kind + 1) * ROWS][sides[h]]
            joined = jnp.where(slot_rows % SLOT == GRP, tail, part[:, :wide])
            kinds.append(jnp.concatenate([joined, part[:, wide:]], axis=1))
    z = place[2] // (NX * NC * DOCS)
    sign = 1 - 2 * lax.rem(z, 2)
    for k, out in zip(ROUNDS, outs):
        kind = lax.rem(z + NZ + sign * k, NZ) // 2
        picked = kinds[0]
        for t in range(1, TYPES):
            picked = jnp.where(kind == t, kinds[t], picked)
        out[...] = picked.astype(BF16)


def token_body(
    place, grad_score, attn, query_rows, grad_rows, own, near, near_other, w0, w1, w2, w3, out, done
):
    shard = own.shape[0]
    probs = attn[...].astype(BF16)
    sides = [slice(h * SIDE, (h + 1) * SIDE) for h in range(KVH)]
    parts = [dot_tn(grad_score[s, :], query_rows[s, :]) for s in sides]
    parts += [dot_tn(probs[s], grad_rows[s, :]) for s in sides]
    grad_keyval = jnp.concatenate(parts, axis=1).astype(BF16)
    blocks = [
        (block_at(place, 0, shard), own[...]),
        (near_at(place, shard), near[...]),
        (near_other_at(place, shard), near_other[...]),
        (block_at(place, 2, shard), across_block(place, w0, w1, w2, w3)),
    ]
    for at, block in blocks:
        out[:, pl.ds(at, shard)] = dot_nt(grad_keyval, block).astype(BF16)
    done[...] = probs[:SLOT, :HD].astype(F32)


def gather_docs(spread):
    got = lax.all_to_all(spread, "dp", 0, 0, axis_index_groups=CHIPS)
    got = got.reshape(-1, spread.shape[2])
    return got, lax.ppermute(got, "dp", OTHER_CORE)


def outer_body(place, a0, a1, a2, a3, b0, b1, b2, b3, out):
    rows = jnp.concatenate([a[...] for a in (a0, a1, a2, a3, b0, b1, b2, b3)], axis=0)
    count = rows.shape[0]
    to = lax.broadcasted_iota(jnp.int32, (count, count), 0)
    at = lax.broadcasted_iota(jnp.int32, (count, count), 1)
    spread = jnp.where(at == (to // SLOT) * SLOT + GRP, 1.0, 0.0).astype(BF16)
    tails = dot_nn(spread, rows[:, : GRP * HD])
    slot = lax.broadcasted_iota(jnp.int32, (count, HD), 0) % SLOT
    heads = jnp.zeros((count, HD), F32)
    for g in range(GRP):
        heads = jnp.where(slot == g, tails[:, g * HD : (g + 1) * HD], heads)
    slots = lax.broadcasted_iota(jnp.int32, (HD // NC, HD), 0)
    cols = lax.broadcasted_iota(jnp.int32, (HD // NC, HD), 1)
    cell = HD // (2 * NX * NC)
    chosen = cols == ((slots // cell) * NC + place[1]) * cell + slots % cell
    chosen = jnp.where(chosen, 1.0, 0.0).astype(BF16)
    left = dot_nt(chosen, heads.astype(BF16)).astype(BF16)
    out[...] = dot_nn(left, rows).astype(BF16)


def exchange_types(factors):
    moved = [lax.ppermute(a, "dp", parity_shift(k)) for a, k in zip(factors[1:], ROUNDS[1:])]
    return [factors[0], *moved]


def reduce_weight(quads, place):
    swapped = [lax.ppermute(a, "dp", OTHER_CORE) for a in quads]
    width = quads[0].shape[1]
    (part,) = call(outer_body, (place,), (*quads, *swapped), [((HD // NC, width), BF16)])
    pieces = part.reshape(2 * NX * NY, -1, width)
    got = lax.all_to_all(pieces, ("dp", "fsdp"), 0, 0, axis_index_groups=OWNERS)
    return jnp.sum(got.astype(F32), axis=0).T


def local(tokens, lengths, queries, positives, kv_weight):
    docs, block, width = tokens.shape[1:]
    shard = kv_weight.shape[0]
    count = docs * block
    dp = lax.axis_index("dp")
    core = dp % NC
    parity = (dp // NC) % 2
    y = lax.axis_index("fsdp")
    place = jnp.stack([y, core, dp * docs, parity]).astype(jnp.int32)
    rows = tokens.reshape(count, width)
    swap = lambda a: lax.ppermute(a, "dp", OTHER_CORE)

    piece = lax.dynamic_slice(kv_weight, (0, (2 * core + parity) * HD), (shard, HD))
    mine = lax.ppermute(piece, "fsdp", Y_ACROSS)
    near = lax.ppermute(tie(kv_weight, mine), ("dp", "fsdp"), y_mirror())
    mate = lax.ppermute(mine, "dp", X_MATE)

    flops = 2 * count * shard * KVW
    part, query_rows = call(
        own_body, (place,), (rows, kv_weight, queries[0]),
        [((count, KVW), F32), ((ROWS, HD), BF16)], [pltpu.VMEM((ROWS, HD), F32)], flops=flops, limit=8,
    )
    near = tie(near, mate, part)
    across = (mine, mate, swap(mine), swap(mate))
    near_other = swap(near)
    (part,) = call(near_body, (place,), (rows, near, part), [((count, KVW), F32)], flops=flops, limit=8)
    keyval, attn, spread, unit, norm = call(
        attend_body,
        (place, lengths[0], positives[0]),
        (rows, part, near_other, *across, query_rows),
        [
            ((count, KVW), BF16),
            ((ROWS, count), F32),
            ((NZ * NX, FOLD * docs, 2 * (HALF + HD) // FOLD), BF16),
            ((SLOT, QW), F32),
            ((SLOT, HD), F32),
        ],
        [pltpu.VMEM((SLOT, QW), F32)],
        flops=2 * flops,
        limit=16,
    )
    everyone = gather_docs(spread)
    loss, grad_score, grad_rows, grad_query, grad_read = call(
        contrast_body,
        (place,),
        (attn, keyval, unit, norm, *everyone),
        [
            ((1, HD), F32),
            ((ROWS, count), BF16),
            ((ROWS, HD), BF16),
            ((docs, QW), BF16),
            ((SLOT, QW), F32),
        ],
        [pltpu.VMEM((ROWS, HD), F32), pltpu.VMEM((SLOT, QW), F32)],
        flops=6_000_000_000,
        limit=8,
    )
    factors = call(
        factor_body,
        (place,),
        (rows, grad_score, attn, queries[0], grad_read),
        [((SIDE, width), BF16)] * len(ROUNDS),
        flops=4 * ROWS * width * count,
        limit=8,
    )
    quads = exchange_types(factors)
    grad_tok, done = call(
        token_body,
        (place,),
        (grad_score, attn, query_rows, grad_rows, kv_weight, near, near_other, *across),
        [((count, width), BF16), ((SLOT, HD), F32)],
        flops=4 * flops,
        limit=20,
    )
    quads = [quads[0], *[tie(a, done) for a in quads[1:]]]
    grad_weight = reduce_weight(quads, place)
    return (loss[:, :docs], grad_tok.reshape(tokens.shape), grad_query[None], grad_weight)


def solution(mesh):
    placed = (
        P("fsdp", "dp", None, None),
        P("fsdp", "dp"),
        P("fsdp", "dp", None),
        P("fsdp", "dp"),
        P("fsdp", None),
    )
    return jax.shard_map(
        local,
        mesh=mesh,
        in_specs=placed,
        out_specs=(
            P("fsdp", "dp"),
            P("fsdp", "dp", None, None),
            P("fsdp", "dp", None),
            P(None, ("dp", "fsdp")),
        ),
        check_vma=False,
    )
```

```python
import jax
import jax.numpy as jnp
from jax import lax
from jax.experimental import pallas as pl
from jax.experimental.pallas import tpu as pltpu
from jax.sharding import PartitionSpec as P

QH = 14
KVH = 2
GRP = QH // KVH
SLOT = 8
HD = 128
QW = QH * HD
KVW = 2 * KVH * HD
HALF = QW // 2
TYPES = 2 * KVH
DOCS = 2
SIDE = DOCS * SLOT
ROWS = KVH * SIDE
FOLD = 4
ROUNDS = (0, -1, -3, 2)
SOFTMAX_TEMPER = 0.05

NZ, NX, NC, NY = 8, 4, 2, 4
N_DP = NZ * NX * NC

F32 = jnp.float32
BF16 = jnp.bfloat16


def dp_index(z, x, c):
    return (z * NX + x) * NC + c


OTHER_CORE = [(i, i ^ 1) for i in range(N_DP)]
CHIPS = [[dp_index(z, x, c) for z in range(NZ) for x in range(NX)] for c in range(NC)]


Y_ACROSS = [(i, (i + 2) % NY) for i in range(NY)]


def x_shift(k):
    return [
        (dp_index(z, x, c), dp_index(z, (x + k) % NX, c))
        for z in range(NZ)
        for x in range(NX)
        for c in range(NC)
    ]


def y_mirror():
    return [
        (dp * NY + y, dp * NY + (y + (1 if dp % NC else NY - 1)) % NY)
        for dp in range(N_DP)
        for y in range(NY)
    ]


OWNERS = [
    [
        dp_index(2 * t + p, x, c) * NY + y
        for p in range(2)
        for x in range(NX)
        for y in range(NY)
    ]
    for t in range(TYPES)
    for c in range(NC)
]


def parity_shift(k):
    pairs = []
    for z in range(NZ):
        to = (z + (k if z % 2 == 0 else -k)) % NZ
        pairs += [(dp_index(z, x, c), dp_index(to, x, c)) for x in range(NX) for c in range(NC)]
    return pairs


def dot_nn(a, b):
    return jnp.dot(a, b, preferred_element_type=F32)


def tie(a, *after):
    return lax.optimization_barrier((a, *after))[0]


def dot_tn(a, b):
    return lax.dot_general(a, b, (((0,), (0,)), ((), ())), preferred_element_type=F32)


def dot_nt(a, b):
    return lax.dot_general(a, b, (((1,), (1,)), ((), ())), preferred_element_type=F32)


def call(body, scalars, arrays, outs, scratch=(), flops=0, limit=4):
    smem = [pl.BlockSpec(memory_space=pltpu.SMEM)] * len(scalars)
    vmem = [pl.BlockSpec(memory_space=pltpu.VMEM)] * len(arrays)
    return pl.pallas_call(
        body,
        out_shape=[jax.ShapeDtypeStruct(s, d) for s, d in outs],
        in_specs=smem + vmem,
        out_specs=[pl.BlockSpec(memory_space=pltpu.VMEM)] * len(outs),
        scratch_shapes=list(scratch),
        compiler_params=pltpu.CompilerParams(vmem_limit_bytes=limit * 1024 * 1024),
        cost_estimate=pl.CostEstimate(flops=flops, bytes_accessed=0, transcendentals=0),
    )(*scalars, *arrays)


def row_mask(lens, block):
    rows = lax.broadcasted_iota(jnp.int32, (ROWS, DOCS * block), 0)
    cols = lax.broadcasted_iota(jnp.int32, (ROWS, DOCS * block), 1)
    row_doc = (rows // SLOT) % DOCS
    length = jnp.where(row_doc == 0, lens[0], lens[1])
    at = cols - row_doc * block
    return (at >= 0) & (at < length)


def block_at(place, k, shard):
    return pl.multiple_of(lax.rem(place[0] + k, NY) * shard, shard)


def near_at(place, shard):
    return block_at(place, jnp.where(place[1] == 0, 1, NY - 1), shard)


def near_other_at(place, shard):
    return block_at(place, jnp.where(place[1] == 0, NY - 1, 1), shard)


def half_body(place, a0, a1, a2, a3, out):
    rows = a0.shape[0]
    for k, piece in enumerate((a0, a1, a2, a3)):
        source = lax.rem(place[3] + NX - k, NX)
        at = pl.multiple_of((source // KVH) * rows, rows)
        lane = pl.multiple_of(lax.rem(source, KVH) * HD, HD)
        out[pl.ds(at, rows), pl.ds(lane, HD)] = piece[...]


def across_block(place, half, half_other):
    first = place[1] == 0
    a, b = half[...], half_other[...]
    return jnp.concatenate([jnp.where(first, a, b), jnp.where(first, b, a)], axis=1)


def own_body(place, tokens, weight, out):
    shard = weight.shape[0]
    out[...] = dot_nn(tokens[:, pl.ds(block_at(place, 0, shard), shard)], weight[...])


def near_body(place, tokens, weight, half, half_other, before, out):
    shard = weight.shape[0]
    across = across_block(place, half, half_other)
    part = dot_nn(tokens[:, pl.ds(near_at(place, shard), shard)], weight[...])
    part += dot_nn(tokens[:, pl.ds(block_at(place, 2, shard), shard)], across)
    out[...] = before[...] + part


def from_lanes(a, out):
    out[...] = jnp.zeros_like(out)
    for kvh in range(KVH):
        for doc in range(DOCS):
            for g in range(GRP):
                i = kvh * GRP + g
                r = kvh * SIDE + doc * SLOT + g
                out[r : r + 1, :] = a[doc : doc + 1, i * HD : (i + 1) * HD]


def to_lanes(rows, kvh, out):
    for doc in range(DOCS):
        for g in range(GRP):
            head = kvh * GRP + g
            r = doc * SLOT + g
            out[doc : doc + 1, head * HD : (head + 1) * HD] = rows[r : r + 1]


def head(a, i):
    return a[:, i * HD : (i + 1) * HD]


def attend_body(
    place, lens, marks, tokens, before, near_other, queries,
    keyval, attn, spread, unit, norm, rows, flat, lined,
):
    shard = near_other.shape[0]
    part = dot_nn(tokens[:, pl.ds(near_other_at(place, shard), shard)], near_other[...])
    total = before[...] + part
    both = total.astype(BF16)
    keyval[...] = both
    from_lanes(queries[...].astype(F32), lined)
    query_rows = lined[...].astype(BF16)
    rows[...] = query_rows
    scores = jnp.concatenate(
        [dot_nt(query_rows[h * SIDE : (h + 1) * SIDE], head(both, h)) for h in range(KVH)], axis=0
    ) * HD ** (-0.5)
    mask = row_mask(lens, both.shape[0] // DOCS)
    expvals = jnp.where(mask, jnp.exp(jnp.where(mask, scores, 0.0)), 0.0)
    probs = expvals / jnp.sum(expvals, axis=-1, keepdims=True)
    attn[...] = probs
    probs = probs.astype(BF16)
    flat[...] = jnp.zeros_like(flat)
    for h in range(KVH):
        to_lanes(dot_nn(probs[h * SIDE : (h + 1) * SIDE], head(both, KVH + h)), h, flat)
    readout = flat[...]
    length = jnp.sqrt(jnp.sum(readout * readout, axis=-1, keepdims=True) + 1e-06)
    vec = readout / length
    unit[...] = vec
    norm[...] = jnp.broadcast_to(length, norm.shape)
    doc_at = lax.broadcasted_iota(jnp.int32, (SLOT, HD), 0)
    mark = jnp.where(doc_at == 0, marks[0], marks[1]).astype(F32)
    whole = jnp.concatenate([vec[:, :HALF], mark, vec[:, HALF:], mark], axis=1)
    wide = spread.shape[2]
    parts = [whole[:DOCS, i * wide : (i + 1) * wide] for i in range(FOLD)]
    folded = jnp.concatenate(parts, axis=0).astype(BF16)
    spread[...] = jnp.broadcast_to(folded[None], spread.shape)


def doc_ids(place, slots, half_docs):
    core = jnp.where(slots < half_docs, place[1], 1 - place[1])
    own = slots % half_docs
    return (own // DOCS) * (NC * DOCS) + core * DOCS + own % DOCS


def contrast_body(
    place, attn, keyval, unit, norm, mine, other,
    loss, grad_score, grad_rows, grad_read, flat,
):
    half_docs = mine.shape[0] // FOLD
    total_docs = NC * half_docs
    count = mine.shape[0]
    to = lax.broadcasted_iota(jnp.int32, (count, count), 0)
    at = lax.broadcasted_iota(jnp.int32, (count, count), 1)
    doc = to % half_docs
    base = (doc // DOCS) * (FOLD * DOCS) + (to // half_docs) * DOCS + doc % DOCS
    order = jnp.where(at == base, 1.0, 0.0).astype(BF16)

    def unfold(a):
        rows = dot_nn(order, a[...])
        parts = [rows[i * half_docs : (i + 1) * half_docs] for i in range(FOLD)]
        return jnp.concatenate(parts, axis=1)

    gathered = jnp.concatenate([unfold(mine), unfold(other)], axis=0)
    span = HALF + HD
    everyone = jnp.concatenate([gathered[:, :HALF], gathered[:, span : span + HALF]], axis=1)
    everyone = everyone.astype(BF16)
    marks = gathered[:, HALF:span]
    ids = lax.broadcasted_iota(jnp.int32, (total_docs, total_docs), 0)
    cols = lax.broadcasted_iota(jnp.int32, (total_docs, total_docs), 1)
    sim = dot_nt(everyone, everyone) / SOFTMAX_TEMPER
    sim_exp = jnp.where(ids == cols, 0.0, jnp.exp(sim))
    total = jnp.sum(sim_exp, axis=-1, keepdims=True)
    picked = marks == doc_ids(place, cols, half_docs).astype(F32)
    all_loss = jnp.log(total) - jnp.sum(jnp.where(picked, sim, 0.0), axis=-1, keepdims=True)
    prob = (sim_exp / total).astype(BF16)
    pick = jnp.where(picked, 1.0, 0.0).astype(BF16)
    at = (place[2] // (NC * DOCS)) * DOCS
    slots = lax.broadcasted_iota(jnp.int32, (SLOT, total_docs), 0)
    here = lax.broadcasted_iota(jnp.int32, (SLOT, total_docs), 1)
    chosen = (here == at + slots) & (slots < DOCS)
    own_rows = jnp.where(chosen, 1.0, 0.0).astype(BF16)
    lane = lax.broadcasted_iota(jnp.int32, (total_docs, HD), 0)
    slot = lax.broadcasted_iota(jnp.int32, (total_docs, HD), 1)
    loss[...] = jnp.sum(jnp.where(lane == at + slot, all_loss, 0.0), axis=0, keepdims=True)
    coef = jnp.concatenate(
        [
            dot_nn(own_rows, prob),
            dot_nt(own_rows, prob),
            dot_nn(own_rows, pick),
            dot_nt(own_rows, pick),
        ],
        axis=0,
    ).astype(BF16)
    parts = dot_nn(coef, everyone)
    grad_unit = (parts[:8] + parts[8:16] - parts[16:24] - parts[24:]) / SOFTMAX_TEMPER
    vec = unit[...]
    along = jnp.sum(vec * grad_unit, axis=-1, keepdims=True)
    full = (grad_unit - vec * along) / norm[:, :1]
    grad_read[...] = full
    from_lanes(full, flat)
    heads = flat[...].astype(BF16)
    grad_rows[...] = heads
    sides = [slice(h * SIDE, (h + 1) * SIDE) for h in range(KVH)]
    grad_w = jnp.concatenate(
        [dot_nt(heads[sides[h]], head(keyval, KVH + h)) for h in range(KVH)], axis=0
    )
    probs = attn[...]
    inner = jnp.sum(probs * grad_w, axis=-1, keepdims=True)
    score = (probs * (grad_w - inner) * HD ** (-0.5)).astype(BF16)
    grad_score[...] = score


def factor_body(place, tokens, grad_score, attn, queries, grad_read, *outs):
    sides = [slice(h * SIDE, (h + 1) * SIDE) for h in range(KVH)]
    wide = GRP * HD
    slot_rows = lax.broadcasted_iota(jnp.int32, (SIDE, wide), 0)
    both = jnp.concatenate([grad_score[...], attn[...].astype(BF16)], axis=0)
    mixed = dot_nn(both, tokens[...])
    tails = [queries[...].astype(F32), grad_read[...]]
    kinds = []
    for kind in range(2):
        for h in range(KVH):
            tail = tails[kind][:, h * wide : (h + 1) * wide]
            tail = jnp.where(slot_rows < SLOT, tail[0:1], tail[1:2])
            part = mixed[kind * ROWS : (kind + 1) * ROWS][sides[h]]
            joined = jnp.where(slot_rows % SLOT == GRP, tail, part[:, :wide])
            kinds.append(jnp.concatenate([joined, part[:, wide:]], axis=1))
    z = place[2] // (NX * NC * DOCS)
    sign = 1 - 2 * lax.rem(z, 2)
    for k, out in zip(ROUNDS, outs):
        kind = lax.rem(z + NZ + sign * k, NZ) // 2
        picked = kinds[0]
        for t in range(1, TYPES):
            picked = jnp.where(kind == t, kinds[t], picked)
        out[...] = picked.astype(BF16)


def token_body(
    place, grad_score, attn, query_rows, grad_rows, keyval, own, near, near_other, half, half_other,
    out, grad_query, done, lanes,
):
    shard = own.shape[0]
    probs = attn[...].astype(BF16)
    sides = [slice(h * SIDE, (h + 1) * SIDE) for h in range(KVH)]
    parts = [dot_tn(grad_score[s, :], query_rows[s, :]) for s in sides]
    parts += [dot_tn(probs[s], grad_rows[s, :]) for s in sides]
    grad_keyval = jnp.concatenate(parts, axis=1).astype(BF16)
    blocks = [
        (block_at(place, 0, shard), own[...]),
        (near_at(place, shard), near[...]),
        (near_other_at(place, shard), near_other[...]),
        (block_at(place, 2, shard), across_block(place, half, half_other)),
    ]
    for at, block in blocks:
        out[:, pl.ds(at, shard)] = dot_nt(grad_keyval, block).astype(BF16)
    lanes[...] = jnp.zeros_like(lanes)
    for h in range(KVH):
        to_lanes(dot_nn(grad_score[sides[h], :], head(keyval, h)), h, lanes)
    grad_query[...] = lanes[:DOCS, :].astype(BF16)
    done[...] = probs[:SLOT, :HD].astype(F32)


def gather_docs(spread):
    got = lax.all_to_all(spread, "dp", 0, 0, axis_index_groups=CHIPS)
    got = got.reshape(-1, spread.shape[2])
    return got, lax.ppermute(got, "dp", OTHER_CORE)


def outer_body(place, a0, a1, a2, a3, b0, b1, b2, b3, out):
    rows = jnp.concatenate([a[...] for a in (a0, a1, a2, a3, b0, b1, b2, b3)], axis=0)
    count = rows.shape[0]
    to = lax.broadcasted_iota(jnp.int32, (count, count), 0)
    at = lax.broadcasted_iota(jnp.int32, (count, count), 1)
    spread = jnp.where(at == (to // SLOT) * SLOT + GRP, 1.0, 0.0).astype(BF16)
    tails = dot_nn(spread, rows[:, : GRP * HD])
    slot = lax.broadcasted_iota(jnp.int32, (count, HD), 0) % SLOT
    heads = jnp.zeros((count, HD), F32)
    for g in range(GRP):
        heads = jnp.where(slot == g, tails[:, g * HD : (g + 1) * HD], heads)
    slots = lax.broadcasted_iota(jnp.int32, (HD // NC, HD), 0)
    cols = lax.broadcasted_iota(jnp.int32, (HD // NC, HD), 1)
    cell = HD // (2 * NX * NC)
    chosen = cols == ((slots // cell) * NC + place[1]) * cell + slots % cell
    chosen = jnp.where(chosen, 1.0, 0.0).astype(BF16)
    left = dot_nt(chosen, heads.astype(BF16)).astype(BF16)
    out[...] = dot_nn(left, rows).astype(BF16)


def exchange_types(factors):
    moved = [lax.ppermute(a, "dp", parity_shift(k)) for a, k in zip(factors[1:], ROUNDS[1:])]
    return [factors[0], *moved]


def reduce_weight(quads, place):
    swapped = [lax.ppermute(a, "dp", OTHER_CORE) for a in quads]
    width = quads[0].shape[1]
    (part,) = call(outer_body, (place,), (*quads, *swapped), [((HD // NC, width), BF16)])
    pieces = part.reshape(2 * NX * NY, -1, width)
    got = lax.all_to_all(pieces, ("dp", "fsdp"), 0, 0, axis_index_groups=OWNERS)
    return jnp.sum(got.astype(F32), axis=0).T


def local(tokens, lengths, queries, positives, kv_weight):
    docs, block, width = tokens.shape[1:]
    shard = kv_weight.shape[0]
    count = docs * block
    dp = lax.axis_index("dp")
    core = dp % NC
    x = (dp // NC) % NX
    y = lax.axis_index("fsdp")
    place = jnp.stack([y, core, dp * docs, x]).astype(jnp.int32)
    rows = tokens.reshape(count, width)
    swap = lambda a: lax.ppermute(a, "dp", OTHER_CORE)

    flops = 2 * count * shard * KVW
    (part,) = call(
        own_body, (place,), (rows, kv_weight), [((count, KVW), F32)], flops=flops, limit=8
    )
    piece = lax.dynamic_slice(
        kv_weight, ((x // KVH) * (shard // 2), (KVH * core + x % KVH) * HD), (shard // 2, HD)
    )
    mine = tie(lax.ppermute(piece, "fsdp", Y_ACROSS), part)
    near = lax.ppermute(tie(kv_weight, mine), ("dp", "fsdp"), y_mirror())
    pieces = [mine] + [lax.ppermute(mine, "dp", x_shift(k)) for k in (1, 2, 3)]
    (half,) = call(half_body, (place,), pieces, [((shard, KVH * HD), BF16)])
    half_other = swap(half)

    near = tie(near, half_other)
    near_other = swap(near)
    (part,) = call(
        near_body, (place,), (rows, near, half, half_other, part), [((count, KVW), F32)],
        flops=2 * flops, limit=8,
    )
    keyval, attn, spread, unit, norm, query_rows = call(
        attend_body,
        (place, lengths[0], positives[0]),
        (rows, part, near_other, queries[0]),
        [
            ((count, KVW), BF16),
            ((ROWS, count), F32),
            ((NZ * NX, FOLD * docs, 2 * (HALF + HD) // FOLD), BF16),
            ((SLOT, QW), F32),
            ((SLOT, HD), F32),
            ((ROWS, HD), BF16),
        ],
        [pltpu.VMEM((SLOT, QW), F32), pltpu.VMEM((ROWS, HD), F32)],
        flops=2 * flops,
        limit=16,
    )
    everyone = gather_docs(spread)
    loss, grad_score, grad_rows, grad_read = call(
        contrast_body,
        (place,),
        (attn, keyval, unit, norm, *everyone),
        [
            ((1, HD), F32),
            ((ROWS, count), BF16),
            ((ROWS, HD), BF16),
            ((SLOT, QW), F32),
        ],
        [pltpu.VMEM((ROWS, HD), F32)],
        flops=6_000_000_000,
        limit=8,
    )
    factors = call(
        factor_body,
        (place,),
        (rows, grad_score, attn, queries[0], grad_read),
        [((SIDE, width), BF16)] * len(ROUNDS),
        flops=4 * ROWS * width * count,
        limit=8,
    )
    quads = exchange_types(factors)
    grad_tok, grad_query, done = call(
        token_body,
        (place,),
        (grad_score, attn, query_rows, grad_rows, keyval, kv_weight, near, near_other, half, half_other),
        [((count, width), BF16), ((docs, QW), BF16), ((SLOT, HD), F32)],
        [pltpu.VMEM((SLOT, QW), F32)],
        flops=4 * flops,
        limit=20,
    )
    quads = [quads[0], *[tie(a, done) for a in quads[1:]]]
    grad_weight = reduce_weight(quads, place)
    return (loss[:, :docs], grad_tok.reshape(tokens.shape), grad_query[None], grad_weight)


def solution(mesh):
    placed = (
        P("fsdp", "dp", None, None),
        P("fsdp", "dp"),
        P("fsdp", "dp", None),
        P("fsdp", "dp"),
        P("fsdp", None),
    )
    return jax.shard_map(
        local,
        mesh=mesh,
        in_specs=placed,
        out_specs=(
            P("fsdp", "dp"),
            P("fsdp", "dp", None, None),
            P("fsdp", "dp", None),
            P(None, ("dp", "fsdp")),
        ),
        check_vma=False,
    )
```

```python
import jax
import jax.numpy as jnp
from jax import lax
from jax.experimental import pallas as pl
from jax.experimental.pallas import tpu as pltpu
from jax.sharding import PartitionSpec as P

QH = 14
KVH = 2
GRP = QH // KVH
SLOT = 8
HD = 128
QW = QH * HD
KVW = 2 * KVH * HD
HALF = QW // 2
TYPES = 2 * KVH
DOCS = 2
SIDE = DOCS * SLOT
ROWS = KVH * SIDE
FOLD = 4
ROUNDS = (0, -1, -3, 2)
SOFTMAX_TEMPER = 0.05

NZ, NX, NC, NY = 8, 4, 2, 4
N_DP = NZ * NX * NC

F32 = jnp.float32
BF16 = jnp.bfloat16


def dp_index(z, x, c):
    return (z * NX + x) * NC + c


OTHER_CORE = [(i, i ^ 1) for i in range(N_DP)]
CHIPS = [[dp_index(z, x, c) for z in range(NZ) for x in range(NX)] for c in range(NC)]


Y_ACROSS = [(i, (i + 2) % NY) for i in range(NY)]


def x_shift(k):
    return [
        (dp_index(z, x, c), dp_index(z, (x + k) % NX, c))
        for z in range(NZ)
        for x in range(NX)
        for c in range(NC)
    ]


def y_mirror():
    return [
        (dp * NY + y, dp * NY + (y + (1 if dp % NC else NY - 1)) % NY)
        for dp in range(N_DP)
        for y in range(NY)
    ]


OWNERS = [
    [
        dp_index(2 * t + p, x, c) * NY + y
        for p in range(2)
        for x in range(NX)
        for y in range(NY)
    ]
    for t in range(TYPES)
    for c in range(NC)
]


def parity_shift(k):
    pairs = []
    for z in range(NZ):
        to = (z + (k if z % 2 == 0 else -k)) % NZ
        pairs += [(dp_index(z, x, c), dp_index(to, x, c)) for x in range(NX) for c in range(NC)]
    return pairs


def dot_nn(a, b):
    return jnp.dot(a, b, preferred_element_type=F32)


def tie(a, *after):
    return lax.optimization_barrier((a, *after))[0]


def dot_tn(a, b):
    return lax.dot_general(a, b, (((0,), (0,)), ((), ())), preferred_element_type=F32)


def dot_nt(a, b):
    return lax.dot_general(a, b, (((1,), (1,)), ((), ())), preferred_element_type=F32)


def call(body, scalars, arrays, outs, scratch=(), flops=0, limit=4):
    smem = [pl.BlockSpec(memory_space=pltpu.SMEM)] * len(scalars)
    vmem = [pl.BlockSpec(memory_space=pltpu.VMEM)] * len(arrays)
    return pl.pallas_call(
        body,
        out_shape=[jax.ShapeDtypeStruct(s, d) for s, d in outs],
        in_specs=smem + vmem,
        out_specs=[pl.BlockSpec(memory_space=pltpu.VMEM)] * len(outs),
        scratch_shapes=list(scratch),
        compiler_params=pltpu.CompilerParams(vmem_limit_bytes=limit * 1024 * 1024),
        cost_estimate=pl.CostEstimate(flops=flops, bytes_accessed=0, transcendentals=0),
    )(*scalars, *arrays)


def row_mask(lens, block):
    rows = lax.broadcasted_iota(jnp.int32, (ROWS, DOCS * block), 0)
    cols = lax.broadcasted_iota(jnp.int32, (ROWS, DOCS * block), 1)
    row_doc = (rows // SLOT) % DOCS
    length = jnp.where(row_doc == 0, lens[0], lens[1])
    at = cols - row_doc * block
    return (at >= 0) & (at < length)


def block_at(place, k, shard):
    return pl.multiple_of(lax.rem(place[0] + k, NY) * shard, shard)


def near_at(place, shard):
    return block_at(place, jnp.where(place[1] == 0, 1, NY - 1), shard)


def near_other_at(place, shard):
    return block_at(place, jnp.where(place[1] == 0, NY - 1, 1), shard)


def place_pieces(place, core, pieces, out):
    rows = pieces[0].shape[0]
    for k, piece in enumerate(pieces):
        source = lax.rem(place[3] + NX - k, NX)
        at = pl.multiple_of((source // KVH) * rows, rows)
        lane = pl.multiple_of((core * KVH + lax.rem(source, KVH)) * HD, HD)
        out[pl.ds(at, rows), pl.ds(lane, HD)] = piece[...]


def own_body(place, tokens, weight, out):
    shard = weight.shape[0]
    out[...] = dot_nn(tokens[:, pl.ds(block_at(place, 0, shard), shard)], weight[...])


def near_body(
    place, tokens, weight, a0, a1, a2, a3, b0, b1, b2, b3, before, out, across
):
    shard = weight.shape[0]
    place_pieces(place, place[1], (a0, a1, a2, a3), across)
    place_pieces(place, 1 - place[1], (b0, b1, b2, b3), across)
    part = dot_nn(tokens[:, pl.ds(near_at(place, shard), shard)], weight[...])
    part += dot_nn(tokens[:, pl.ds(block_at(place, 2, shard), shard)], across[...])
    out[...] = before[...] + part


def from_lanes(a, out):
    out[...] = jnp.zeros_like(out)
    for kvh in range(KVH):
        for doc in range(DOCS):
            for g in range(GRP):
                i = kvh * GRP + g
                r = kvh * SIDE + doc * SLOT + g
                out[r : r + 1, :] = a[doc : doc + 1, i * HD : (i + 1) * HD]


def to_lanes(rows, kvh, out):
    for doc in range(DOCS):
        for g in range(GRP):
            head = kvh * GRP + g
            r = doc * SLOT + g
            out[doc : doc + 1, head * HD : (head + 1) * HD] = rows[r : r + 1]


def head(a, i):
    return a[:, i * HD : (i + 1) * HD]


def attend_body(
    place, lens, marks, tokens, before, near_other, queries,
    keyval, attn, spread, unit, norm, rows, flat, lined,
):
    shard = near_other.shape[0]
    part = dot_nn(tokens[:, pl.ds(near_other_at(place, shard), shard)], near_other[...])
    total = before[...] + part
    both = total.astype(BF16)
    keyval[...] = both
    from_lanes(queries[...].astype(F32), lined)
    query_rows = lined[...].astype(BF16)
    rows[...] = query_rows
    scores = jnp.concatenate(
        [dot_nt(query_rows[h * SIDE : (h + 1) * SIDE], head(both, h)) for h in range(KVH)], axis=0
    ) * HD ** (-0.5)
    mask = row_mask(lens, both.shape[0] // DOCS)
    expvals = jnp.where(mask, jnp.exp(jnp.where(mask, scores, 0.0)), 0.0)
    probs = expvals / jnp.sum(expvals, axis=-1, keepdims=True)
    attn[...] = probs
    probs = probs.astype(BF16)
    flat[...] = jnp.zeros_like(flat)
    for h in range(KVH):
        to_lanes(dot_nn(probs[h * SIDE : (h + 1) * SIDE], head(both, KVH + h)), h, flat)
    readout = flat[...]
    length = jnp.sqrt(jnp.sum(readout * readout, axis=-1, keepdims=True) + 1e-06)
    vec = readout / length
    unit[...] = vec
    norm[...] = jnp.broadcast_to(length, norm.shape)
    doc_at = lax.broadcasted_iota(jnp.int32, (SLOT, HD), 0)
    mark = jnp.where(doc_at == 0, marks[0], marks[1]).astype(F32)
    whole = jnp.concatenate([vec[:, :HALF], mark, vec[:, HALF:], mark], axis=1)
    wide = spread.shape[2]
    parts = [whole[:DOCS, i * wide : (i + 1) * wide] for i in range(FOLD)]
    folded = jnp.concatenate(parts, axis=0).astype(BF16)
    spread[...] = jnp.broadcast_to(folded[None], spread.shape)


def doc_ids(place, slots, half_docs):
    core = jnp.where(slots < half_docs, place[1], 1 - place[1])
    own = slots % half_docs
    return (own // DOCS) * (NC * DOCS) + core * DOCS + own % DOCS


def contrast_body(
    place, attn, keyval, unit, norm, mine, other,
    loss, grad_score, grad_rows, grad_read, flat,
):
    half_docs = mine.shape[0] // FOLD
    total_docs = NC * half_docs
    count = mine.shape[0]
    to = lax.broadcasted_iota(jnp.int32, (count, count), 0)
    at = lax.broadcasted_iota(jnp.int32, (count, count), 1)
    doc = to % half_docs
    base = (doc // DOCS) * (FOLD * DOCS) + (to // half_docs) * DOCS + doc % DOCS
    order = jnp.where(at == base, 1.0, 0.0).astype(BF16)

    def unfold(a):
        rows = dot_nn(order, a[...])
        parts = [rows[i * half_docs : (i + 1) * half_docs] for i in range(FOLD)]
        return jnp.concatenate(parts, axis=1)

    gathered = jnp.concatenate([unfold(mine), unfold(other)], axis=0)
    span = HALF + HD
    everyone = jnp.concatenate([gathered[:, :HALF], gathered[:, span : span + HALF]], axis=1)
    everyone = everyone.astype(BF16)
    marks = gathered[:, HALF:span]
    ids = lax.broadcasted_iota(jnp.int32, (total_docs, total_docs), 0)
    cols = lax.broadcasted_iota(jnp.int32, (total_docs, total_docs), 1)
    sim = dot_nt(everyone, everyone) / SOFTMAX_TEMPER
    sim_exp = jnp.where(ids == cols, 0.0, jnp.exp(sim))
    total = jnp.sum(sim_exp, axis=-1, keepdims=True)
    picked = marks == doc_ids(place, cols, half_docs).astype(F32)
    all_loss = jnp.log(total) - jnp.sum(jnp.where(picked, sim, 0.0), axis=-1, keepdims=True)
    prob = (sim_exp / total).astype(BF16)
    pick = jnp.where(picked, 1.0, 0.0).astype(BF16)
    at = (place[2] // (NC * DOCS)) * DOCS
    slots = lax.broadcasted_iota(jnp.int32, (SLOT, total_docs), 0)
    here = lax.broadcasted_iota(jnp.int32, (SLOT, total_docs), 1)
    chosen = (here == at + slots) & (slots < DOCS)
    own_rows = jnp.where(chosen, 1.0, 0.0).astype(BF16)
    lane = lax.broadcasted_iota(jnp.int32, (total_docs, HD), 0)
    slot = lax.broadcasted_iota(jnp.int32, (total_docs, HD), 1)
    loss[...] = jnp.sum(jnp.where(lane == at + slot, all_loss, 0.0), axis=0, keepdims=True)
    coef = jnp.concatenate(
        [
            dot_nn(own_rows, prob),
            dot_nt(own_rows, prob),
            dot_nn(own_rows, pick),
            dot_nt(own_rows, pick),
        ],
        axis=0,
    ).astype(BF16)
    parts = dot_nn(coef, everyone)
    grad_unit = (parts[:8] + parts[8:16] - parts[16:24] - parts[24:]) / SOFTMAX_TEMPER
    vec = unit[...]
    along = jnp.sum(vec * grad_unit, axis=-1, keepdims=True)
    full = (grad_unit - vec * along) / norm[:, :1]
    grad_read[...] = full
    from_lanes(full, flat)
    heads = flat[...].astype(BF16)
    grad_rows[...] = heads
    sides = [slice(h * SIDE, (h + 1) * SIDE) for h in range(KVH)]
    grad_w = jnp.concatenate(
        [dot_nt(heads[sides[h]], head(keyval, KVH + h)) for h in range(KVH)], axis=0
    )
    probs = attn[...]
    inner = jnp.sum(probs * grad_w, axis=-1, keepdims=True)
    score = (probs * (grad_w - inner) * HD ** (-0.5)).astype(BF16)
    grad_score[...] = score


def factor_body(place, tokens, grad_score, attn, queries, grad_read, *outs):
    sides = [slice(h * SIDE, (h + 1) * SIDE) for h in range(KVH)]
    wide = GRP * HD
    slot_rows = lax.broadcasted_iota(jnp.int32, (SIDE, wide), 0)
    both = jnp.concatenate([grad_score[...], attn[...].astype(BF16)], axis=0)
    mixed = dot_nn(both, tokens[...])
    tails = [queries[...].astype(F32), grad_read[...]]
    kinds = []
    for kind in range(2):
        for h in range(KVH):
            tail = tails[kind][:, h * wide : (h + 1) * wide]
            tail = jnp.where(slot_rows < SLOT, tail[0:1], tail[1:2])
            part = mixed[kind * ROWS : (kind + 1) * ROWS][sides[h]]
            joined = jnp.where(slot_rows % SLOT == GRP, tail, part[:, :wide])
            kinds.append(jnp.concatenate([joined, part[:, wide:]], axis=1))
    z = place[2] // (NX * NC * DOCS)
    sign = 1 - 2 * lax.rem(z, 2)
    for k, out in zip(ROUNDS, outs):
        kind = lax.rem(z + NZ + sign * k, NZ) // 2
        picked = kinds[0]
        for t in range(1, TYPES):
            picked = jnp.where(kind == t, kinds[t], picked)
        out[...] = picked.astype(BF16)


def token_body(
    place, grad_score, attn, query_rows, grad_rows, keyval, own, near, near_other, across,
    out, grad_query, done, lanes,
):
    shard = own.shape[0]
    probs = attn[...].astype(BF16)
    sides = [slice(h * SIDE, (h + 1) * SIDE) for h in range(KVH)]
    parts = [dot_tn(grad_score[s, :], query_rows[s, :]) for s in sides]
    parts += [dot_tn(probs[s], grad_rows[s, :]) for s in sides]
    grad_keyval = jnp.concatenate(parts, axis=1).astype(BF16)
    blocks = [
        (block_at(place, 0, shard), own[...]),
        (near_at(place, shard), near[...]),
        (near_other_at(place, shard), near_other[...]),
        (block_at(place, 2, shard), across[...]),
    ]
    for at, block in blocks:
        out[:, pl.ds(at, shard)] = dot_nt(grad_keyval, block).astype(BF16)
    lanes[...] = jnp.zeros_like(lanes)
    for h in range(KVH):
        to_lanes(dot_nn(grad_score[sides[h], :], head(keyval, h)), h, lanes)
    grad_query[...] = lanes[:DOCS, :].astype(BF16)
    done[...] = probs[:SLOT, :HD].astype(F32)


def gather_docs(spread):
    got = lax.all_to_all(spread, "dp", 0, 0, axis_index_groups=CHIPS)
    got = got.reshape(-1, spread.shape[2])
    return got, lax.ppermute(got, "dp", OTHER_CORE)


def outer_body(place, a0, a1, a2, a3, b0, b1, b2, b3, out):
    rows = jnp.concatenate([a[...] for a in (a0, a1, a2, a3, b0, b1, b2, b3)], axis=0)
    count = rows.shape[0]
    to = lax.broadcasted_iota(jnp.int32, (count, count), 0)
    at = lax.broadcasted_iota(jnp.int32, (count, count), 1)
    spread = jnp.where(at == (to // SLOT) * SLOT + GRP, 1.0, 0.0).astype(BF16)
    tails = dot_nn(spread, rows[:, : GRP * HD])
    slot = lax.broadcasted_iota(jnp.int32, (count, HD), 0) % SLOT
    heads = jnp.zeros((count, HD), F32)
    for g in range(GRP):
        heads = jnp.where(slot == g, tails[:, g * HD : (g + 1) * HD], heads)
    slots = lax.broadcasted_iota(jnp.int32, (HD // NC, HD), 0)
    cols = lax.broadcasted_iota(jnp.int32, (HD // NC, HD), 1)
    cell = HD // (2 * NX * NC)
    chosen = cols == ((slots // cell) * NC + place[1]) * cell + slots % cell
    chosen = jnp.where(chosen, 1.0, 0.0).astype(BF16)
    left = dot_nt(chosen, heads.astype(BF16)).astype(BF16)
    out[...] = dot_nn(left, rows).astype(BF16)


def exchange_types(factors):
    moved = [lax.ppermute(a, "dp", parity_shift(k)) for a, k in zip(factors[1:], ROUNDS[1:])]
    return [factors[0], *moved]


def reduce_weight(quads, place):
    swapped = [lax.ppermute(a, "dp", OTHER_CORE) for a in quads]
    width = quads[0].shape[1]
    (part,) = call(outer_body, (place,), (*quads, *swapped), [((HD // NC, width), BF16)])
    pieces = part.reshape(2 * NX * NY, -1, width)
    got = lax.all_to_all(pieces, ("dp", "fsdp"), 0, 0, axis_index_groups=OWNERS)
    return jnp.sum(got.astype(F32), axis=0).T


def local(tokens, lengths, queries, positives, kv_weight):
    docs, block, width = tokens.shape[1:]
    shard = kv_weight.shape[0]
    count = docs * block
    dp = lax.axis_index("dp")
    core = dp % NC
    x = (dp // NC) % NX
    y = lax.axis_index("fsdp")
    place = jnp.stack([y, core, dp * docs, x]).astype(jnp.int32)
    rows = tokens.reshape(count, width)
    swap = lambda a: lax.ppermute(a, "dp", OTHER_CORE)

    flops = 2 * count * shard * KVW
    (part,) = call(
        own_body, (place,), (rows, kv_weight), [((count, KVW), F32)], flops=flops, limit=8
    )
    piece = lax.dynamic_slice(
        kv_weight, ((x // KVH) * (shard // 2), (KVH * core + x % KVH) * HD), (shard // 2, HD)
    )
    mine = tie(lax.ppermute(piece, "fsdp", Y_ACROSS), part)
    near = lax.ppermute(tie(kv_weight, mine), ("dp", "fsdp"), y_mirror())
    pieces = [mine] + [lax.ppermute(mine, "dp", x_shift(k)) for k in (1, 2, 3)]
    swapped = [swap(a) for a in pieces]
    near = tie(near, *swapped)
    near_other = swap(near)
    part, across = call(
        near_body, (place,), (rows, near, *pieces, *swapped, part),
        [((count, KVW), F32), ((shard, KVW), BF16)],
        flops=2 * flops, limit=8,
    )
    keyval, attn, spread, unit, norm, query_rows = call(
        attend_body,
        (place, lengths[0], positives[0]),
        (rows, part, near_other, queries[0]),
        [
            ((count, KVW), BF16),
            ((ROWS, count), F32),
            ((NZ * NX, FOLD * docs, 2 * (HALF + HD) // FOLD), BF16),
            ((SLOT, QW), F32),
            ((SLOT, HD), F32),
            ((ROWS, HD), BF16),
        ],
        [pltpu.VMEM((SLOT, QW), F32), pltpu.VMEM((ROWS, HD), F32)],
        flops=2 * flops,
        limit=16,
    )
    everyone = gather_docs(spread)
    loss, grad_score, grad_rows, grad_read = call(
        contrast_body,
        (place,),
        (attn, keyval, unit, norm, *everyone),
        [
            ((1, HD), F32),
            ((ROWS, count), BF16),
            ((ROWS, HD), BF16),
            ((SLOT, QW), F32),
        ],
        [pltpu.VMEM((ROWS, HD), F32)],
        flops=6_000_000_000,
        limit=8,
    )
    factors = call(
        factor_body,
        (place,),
        (rows, grad_score, attn, queries[0], grad_read),
        [((SIDE, width), BF16)] * len(ROUNDS),
        flops=4 * ROWS * width * count,
        limit=8,
    )
    quads = exchange_types(factors)
    grad_tok, grad_query, done = call(
        token_body,
        (place,),
        (grad_score, attn, query_rows, grad_rows, keyval, kv_weight, near, near_other, across),
        [((count, width), BF16), ((docs, QW), BF16), ((SLOT, HD), F32)],
        [pltpu.VMEM((SLOT, QW), F32)],
        flops=4 * flops,
        limit=20,
    )
    quads = [quads[0], *[tie(a, done) for a in quads[1:]]]
    grad_weight = reduce_weight(quads, place)
    return (loss[:, :docs], grad_tok.reshape(tokens.shape), grad_query[None], grad_weight)


def solution(mesh):
    placed = (
        P("fsdp", "dp", None, None),
        P("fsdp", "dp"),
        P("fsdp", "dp", None),
        P("fsdp", "dp"),
        P("fsdp", None),
    )
    return jax.shard_map(
        local,
        mesh=mesh,
        in_specs=placed,
        out_specs=(
            P("fsdp", "dp"),
            P("fsdp", "dp", None, None),
            P("fsdp", "dp", None),
            P(None, ("dp", "fsdp")),
        ),
        check_vma=False,
    )
```
